32 devices in a mesh: order: 4 (over y, core), basin: 8 (over z, x).
Axes of the slice: x: 2, y: 2, z: 4, core: 2. Of those that a mesh axis runs over, the one named last changes fastest.
Arguments:
- forcings: bfloat16 [32, 16, 16384], P(None, None, ('order', 'basin')), may hold values from -6 to 6
- w_input: bfloat16 [512, 16], replicated, may hold values from -1.5 to 1.5
- w_recur: bfloat16 [512, 128], replicated, may hold values from -0.5 to 0.5
- gate_bias: float32 [512], replicated, may hold values from -3 to 3
- w_runoff: float32 [128], replicated, may hold values from -0.5 to 0.5
- travel_time: float32 [16384], P(('order', 'basin')), may hold values from 1 to 8
- weight_x: float32 [16384], P(('order', 'basin')), may hold values from 0 to 0.3
- drain_basin: int32 [16384, 1], P(('order', 'basin')), may hold values from 0 to 7; in each aligned block of 512 rows (0 to 511, 512 to 1023, ...) at most 128 rows name the same one
- drain_reach: int32 [16384, 1], P(('order', 'basin')), may hold values from 0 to 511
Outputs:
- discharge: float32 [32, 16384], P(None, ('order', 'basin'))
The draws below stay inside these ranges and needn't reach their ends.
Inputs may be any that keep to these rules, and one draw needn't show every extreme that they name: `drain_basin`: among the reaches of one device (aligned blocks of 512 reaches), at most 128 drain to the same basin index, and exactly 128 do for some basin index in some block.
All inputs are finite; a program needn't handle non-finite values.
Results may differ from the reference program's by a relative error of at most 0.0003.
Values sent between devices are 32-bit elements; how exact they have to be, the bound alone decides.
No kernel may reach another device: no remote copies, remote signals or barrier semaphores. Data moves between devices by JAX's collectives and lax.ppermute only.
A program may use at most 64 MiB of HBM per device.

```python
import math
import jax
import jax.numpy as jnp
import numpy as np
from jax import lax

CHANNELS = 16
UNITS = 128
DAYS = 32
R_DEV = 512
CAP = 128
REACHES = 16384
N_ORDER = 4
N_BASIN = 8


def place_ends(drawn, key, smallest, high):
    longest = drawn.shape.index(max(drawn.shape))
    spots = []
    for shift in (0, 1):
        where = [jax.random.randint(jax.random.fold_in(key, axis), (), 0, length) for axis, length in enumerate(drawn.shape)]
        where[longest] = (where[longest] + shift) % drawn.shape[longest]
        spots.append(tuple(where))
    return drawn.at[spots[0]].set(smallest).at[spots[1]].set(high)


def block_levels(key, dims, cuts, smallest, top_value):
    factor_of = 1.0
    for dim, parts in cuts:
        draws = jax.random.uniform(jax.random.fold_in(jax.random.fold_in(key, 6), dim), (parts,), jnp.float32, smallest / len(cuts), top_value / len(cuts))
        factor_of = factor_of * jnp.repeat(jnp.exp(draws), dims[dim] // parts).reshape((-1,) + (1,) * (len(dims) - 1 - dim))
    return factor_of


def assign_block(stream_key, own, number, rows, amount, top, bound, skew):
    ranking = jax.random.permutation(stream_key, amount)
    heavy_load, ordinary = shares(amount, rows * top, bound, skew, True), shares(amount, rows * top, bound, skew, False)
    places = jnp.arange(amount)

    def named(sizes, offset_by):
        used = int((sizes > 0).sum())
        fixed = max(1, used // 4)
        moved = fixed + (places - fixed + offset_by * (used - fixed)) % max(1, amount - fixed)
        return jnp.zeros((amount,), jnp.int32).at[ranking[jnp.where(places < fixed, places, moved)]].set(jnp.asarray(sizes, jnp.int32))

    sizes = jnp.where(number % 4 == 0, named(heavy_load, number // 4), named(ordinary, number - number // 4 - 1))
    mixed = jax.random.permutation(jax.random.fold_in(own, 3), amount)
    donor, sink = mixed[0:amount // 2 * 2:2], mixed[1:amount // 2 * 2:2]
    room = jnp.minimum(sizes[donor] - 1, bound - sizes[sink]) // 2
    room = jnp.where((donor == ranking[0]) | (sink == ranking[0]) | (sizes[sink] == 0), 0, jnp.maximum(room, 0))
    moved = jax.random.randint(jax.random.fold_in(own, 4), (amount // 2,), 0, 1 << 20) % (room + 1)
    sizes = sizes.at[donor].add(-moved).at[sink].add(moved)
    labels = jnp.searchsorted(jnp.cumsum(sizes), jnp.arange(rows * top), side="right").astype(jnp.int32)
    table = labels.reshape(top, rows).T
    table = table[jax.random.permutation(jax.random.fold_in(own, 1), rows)]
    offset_by = jax.random.randint(jax.random.fold_in(own, 2), (rows, 1), 0, top)
    return jnp.take_along_axis(table, (jnp.arange(top)[None, :] + offset_by) % top, axis=1)


def shares(amount, total, limit, lean, full):
    portions = [(1 << 20) // math.isqrt(grade ** lean) + 1 for grade in range(1, amount + 1)]
    largest = limit if full else min(limit, max(-(-total // amount), total * portions[0] // sum(portions)))
    least = 1 if total - largest >= amount - 1 else 0
    counts, surplus = [largest] + [least] * (amount - 1), total - largest - least * (amount - 1)
    while surplus > 0:
        free = [i for i in range(1, amount) if counts[i] < largest] or [i for i in range(1, amount) if counts[i] < limit]
        pool, remaining = sum([portions[i] for i in free]), surplus
        for i in free:
            more = min(limit - counts[i], max(1, remaining * portions[i] // pool), surplus)
            counts[i] = counts[i] + more
            surplus = surplus - more
    return np.array(counts)


def scatter_about(key, extent, scale, bound, split=(), kind=jnp.bfloat16):
    level = block_levels(key, extent, split, -0.22, 0.18) if split else 1.0
    array = jax.random.normal(key, extent, jnp.float32) * scale * level
    return jnp.minimum(jnp.maximum(array, -bound), bound).astype(kind)


def setup_inputs(seed: int = 0) -> dict:
    keys = jax.random.split(jax.random.key(seed), 10)
    forcings = scatter_about(keys[0], (DAYS, CHANNELS, REACHES), 1.0, 6.0, ((2, 32),))
    w_input = scatter_about(keys[1], (4 * UNITS, CHANNELS), CHANNELS ** -0.5, 1.5)
    w_recur = scatter_about(keys[2], (4 * UNITS, UNITS), UNITS ** -0.5, 0.5)
    gate_bias = scatter_about(keys[3], (4 * UNITS,), 1.0, 3.0, (), jnp.float32)
    w_runoff = scatter_about(keys[4], (UNITS,), UNITS ** -0.5, 0.5, (), jnp.float32)
    travel_time = jnp.clip(jnp.exp(math.log(8.0) - 2.0794415 * jax.random.uniform(keys[5], (REACHES,), jnp.float32) ** block_levels(keys[5], (REACHES,), ((0, 32),), -0.2, 0.2)), 1.0, 8.0)
    weight_x = jnp.clip(0.3 * jax.random.uniform(keys[6], (REACHES,), jnp.float32) ** block_levels(keys[6], (REACHES,), ((0, 32),), -0.2, 0.2), 0.0, 0.3)
    drain_basin_keys = jax.random.split(jax.random.fold_in(keys[7], 1), REACHES // R_DEV)
    drain_basin_turns = jax.random.permutation(jax.random.fold_in(keys[7], 3), REACHES // R_DEV)
    drain_basin = jax.vmap(lambda own, number: assign_block(jax.random.fold_in(keys[7], 2), own, number, R_DEV, N_BASIN, 1, CAP, 2))(drain_basin_keys, drain_basin_turns).reshape((REACHES, 1))
    drain_reach = place_ends(jax.random.randint(keys[8], (REACHES, 1), 0, R_DEV), jax.random.fold_in(keys[8], 1), 0, R_DEV - 1).astype(jnp.int32)
    return dict(forcings=forcings, w_input=w_input, w_recur=w_recur, gate_bias=gate_bias, w_runoff=w_runoff, travel_time=travel_time, weight_x=weight_x, drain_basin=drain_basin, drain_reach=drain_reach)


def lstm_days(lstm_state, day_block, w_input, w_recur, gate_bias, w_runoff):
    units = w_recur.shape[1]

    def one_day(recurrent, inputs):
        hidden, memory = recurrent
        gate_sums = jnp.dot(w_input, inputs, preferred_element_type=jnp.float32) + jnp.dot(w_recur, hidden, preferred_element_type=jnp.float32) + gate_bias[:, None]
        ingate = jax.nn.sigmoid(gate_sums[:units])
        forget = jax.nn.sigmoid(gate_sums[units:2 * units])
        candidate = jnp.tanh(gate_sums[2 * units:3 * units])
        outgate = jax.nn.sigmoid(gate_sums[3 * units:])
        memory = forget * memory + ingate * candidate
        hidden = (outgate * jnp.tanh(memory)).astype(jnp.bfloat16)
        runoff = jax.nn.softplus(jnp.dot(w_runoff, hidden.astype(jnp.float32), precision=lax.Precision.HIGHEST))
        return (hidden, memory), runoff

    return lax.scan(one_day, lstm_state, day_block)


def routing_response(travel_time, weight_x, day_count):
    denominator = travel_time * (1.0 - weight_x) + 0.5
    coeff_first = (0.5 - travel_time * weight_x) / denominator
    coeff_second = (0.5 + travel_time * weight_x) / denominator
    recession = (travel_time * (1.0 - weight_x) - 0.5) / denominator
    lag_days = jnp.arange(day_count, dtype=jnp.float32)[:, None]
    later_terms = (coeff_first * recession + coeff_second)[None, :] * jnp.exp((lag_days - 1.0) * jnp.log(recession)[None, :])
    return jnp.where(lag_days < 0.5, coeff_first[None, :], later_terms)


def route(inflow, response):
    length = inflow.shape[0]
    summed = response[0][None, :] * inflow
    for delay in range(1, length):
        shifted = jnp.pad(inflow[:length - delay], ((delay, 0), (0, 0)))
        summed = summed + response[delay][None, :] * shifted
    return summed


def reference(forcings, w_input, w_recur, gate_bias, w_runoff, travel_time, weight_x, drain_basin, drain_reach):
    group_reach = R_DEV * N_BASIN
    day_count = forcings.shape[0]
    per_group = jnp.moveaxis(forcings.reshape(day_count, CHANNELS, N_ORDER, group_reach), 2, 0)
    travels = travel_time.reshape(N_ORDER, group_reach)
    weights = weight_x.reshape(N_ORDER, group_reach)
    target = (drain_basin[:, 0] * R_DEV + drain_reach[:, 0]).astype(jnp.int32).reshape(N_ORDER, group_reach)

    def one_group(arrive, inputs):
        day_block, travel, weighting, target_group = inputs
        lstm_state = (jnp.zeros((UNITS, group_reach), jnp.bfloat16), jnp.zeros((UNITS, group_reach), jnp.float32))
        _, runoff = lstm_days(lstm_state, day_block, w_input, w_recur, gate_bias, w_runoff)
        routed = route(runoff + arrive, routing_response(travel, weighting, day_count))
        passed = jnp.zeros((group_reach, day_count), jnp.float32).at[target_group].add(routed.T).T
        return passed, routed

    _, history = lax.scan(one_group, jnp.zeros((day_count, group_reach), jnp.float32), (per_group, travels, weights, target))
    return jnp.moveaxis(history, 0, 1).reshape(day_count, N_ORDER * group_reach)
```

```python
import functools

import jax
import jax.numpy as jnp
from jax import lax
from jax.experimental import pallas as pl
from jax.experimental.pallas import tpu as pltpu
from jax.sharding import PartitionSpec as P

F32 = jnp.float32
BF16 = jnp.bfloat16
ID_ROWS = 8
CHUNK = 256


def vmem():
    return pl.BlockSpec(memory_space=pltpu.VMEM)


def call(body, out_shape, megabytes=8, **more):
    return pl.pallas_call(
        body,
        out_shape=out_shape,
        out_specs=jax.tree.map(lambda _: vmem(), out_shape),
        compiler_params=pltpu.CompilerParams(vmem_limit_bytes=megabytes << 20),
        **more,
    )


def delayed(series, days):
    return jnp.concatenate(
        [jnp.zeros((days, series.shape[1]), series.dtype), series[: series.shape[0] - days]], axis=0
    )


def routing_coefficients(travel_time, weight_x):
    held = travel_time * (1.0 - weight_x)
    denominator = held + 0.5
    coeff_first = (0.5 - travel_time * weight_x) / denominator
    coeff_second = (0.5 + travel_time * weight_x) / denominator
    recession = (held - 0.5) / denominator
    return coeff_first, coeff_first * recession + coeff_second, recession


def route(inflow, coefficients):
    first, later, recession = coefficients
    stored, power, reach = inflow, recession, 1
    while reach < inflow.shape[0]:
        stored = stored + power * delayed(stored, reach)
        power, reach = power * power, 2 * reach
    return first * inflow + later * delayed(stored, 1)


def in_halves(values):
    high = values.astype(BF16)
    return jnp.concatenate([high, (values - high.astype(F32)).astype(BF16)], axis=0)


def choose(values, table):
    both = jnp.dot(in_halves(values), table, preferred_element_type=F32)
    return both[: values.shape[0]] + both[values.shape[0] :]


def as_column(row):
    return jnp.transpose(jnp.broadcast_to(row, (8, row.shape[1])))[:, :1]


def one_hot(index_column, width):
    lanes = lax.broadcasted_iota(jnp.int32, (index_column.shape[0], width), 1).astype(F32)
    return jnp.where(index_column == lanes, 1.0, 0.0).astype(BF16)


def lay_out(ref, rows, first_row=0):
    count = rows.shape[0]
    if len(ref.shape) == 2:
        ref[first_row : first_row + count, :] = rows
    else:
        capacity = ref.shape[2]
        for basin in range(ref.shape[0]):
            ref[basin, first_row : first_row + count, :] = rows[
                :, basin * capacity : (basin + 1) * capacity
            ]


def take_in(ref, first_row, count):
    if len(ref.shape) == 2:
        return ref[first_row : first_row + count, :]
    return jnp.concatenate(
        [ref[basin, first_row : first_row + count, :] for basin in range(ref.shape[0])], axis=1
    )


def send_slots(drain_to, basins, capacity):
    reaches = drain_to.shape[1]
    basin_rows = max(basins, 8)
    member = (lax.broadcasted_iota(jnp.int32, (basin_rows, reaches), 0) == drain_to).astype(F32)
    before = lax.broadcasted_iota(jnp.int32, (reaches, reaches), 0)
    after = lax.broadcasted_iota(jnp.int32, (reaches, reaches), 1)
    upper = jnp.where(before < after, 1.0, 0.0).astype(BF16)
    earlier = jnp.dot(member.astype(BF16), upper, preferred_element_type=F32)
    rank = jnp.sum(member * earlier, axis=0, keepdims=True)
    return drain_to.astype(F32) * capacity + rank


def first_body(
    forcings_ref,
    w_input_ref,
    w_recur_ref,
    gate_bias_ref,
    w_runoff_ref,
    params_ref,
    drain_ref,
    runoff_ref,
    coefficients_ref,
    send_table_ref,
    outgoing_ref,
    weights,
    sums,
    *,
    days,
    basins,
):
    reaches = forcings_ref.shape[1]
    channels = forcings_ref.shape[0] // days
    units = w_recur_ref.shape[1]
    gates = 4 * units
    per_block = units // channels
    capacity = 2 * reaches // basins

    gate_lane = lax.broadcasted_iota(jnp.int32, (1, gates), 1)
    is_candidate = (gate_lane >= 2 * units) & (gate_lane < 3 * units)
    scale = jnp.where(is_candidate, 1.0, 0.5)
    recur = (jnp.transpose(w_recur_ref[...].astype(F32)) * (0.5 * scale)).astype(BF16)
    inputs = (jnp.transpose(w_input_ref[...].astype(F32)) * scale).astype(BF16)
    bias = gate_bias_ref[...] * scale
    readout = 0.5 * w_runoff_ref[...]
    for day in range(per_block):
        weights[day, :units, :] = recur
        weights[day, units:, :] = jnp.zeros((units, gates), BF16)
        weights[day, units + day * channels : units + (day + 1) * channels, :] = inputs
    sums[...] = jnp.zeros_like(sums)
    chunk = min(CHUNK, reaches)
    chunks = reaches // chunk
    lane = lax.broadcasted_iota(jnp.int32, (chunk, units), 1)

    def block_of_days(block, state):
        rows = pl.ds(pl.multiple_of(block * units, units), units)
        forced = jnp.transpose(forcings_ref[rows, :].astype(F32)).astype(BF16)
        state = list(state)
        for day in range(per_block):
            for part in range(chunks):
                hidden, memory = state[part]
                span = slice(part * chunk, (part + 1) * chunk)
                gate_sums = bias + jnp.dot(
                    jnp.concatenate([hidden, forced[span]], axis=1),
                    weights[day],
                    preferred_element_type=F32,
                )
                ingate = jnp.tanh(gate_sums[:, :units])
                forget = jnp.tanh(gate_sums[:, units : 2 * units])
                candidate = jnp.tanh(gate_sums[:, 2 * units : 3 * units])
                outgate = jnp.tanh(gate_sums[:, 3 * units :])
                memory = 0.5 * ((forget * memory + memory) + (ingate * candidate + candidate))
                squashed = jnp.tanh(memory)
                hidden = (outgate * squashed + squashed).astype(BF16)
                drained = jnp.sum(hidden.astype(F32) * readout, axis=1, keepdims=True)
                sums[span, :] = jnp.where(lane == block * per_block + day, drained, sums[span, :])
                state[part] = (hidden, memory)
        return tuple(state)

    state = tuple(
        (jnp.zeros((chunk, units), BF16), jnp.zeros((chunk, units), F32)) for _ in range(chunks)
    )
    lax.fori_loop(0, days // per_block, block_of_days, state)
    pre = jnp.transpose(sums[...])[:days]
    runoff = jnp.maximum(pre, 0.0) + jnp.log1p(jnp.exp(-jnp.abs(pre)))
    runoff_ref[...] = runoff

    coefficients = routing_coefficients(params_ref[0:1, :], params_ref[1:2, :])
    for row in range(3):
        coefficients_ref[row : row + 1, :] = coefficients[row]
    slots = send_slots(drain_ref[0:1, :], basins, capacity)
    send_table = one_hot(as_column(slots), basins * capacity)
    send_table_ref[...] = send_table
    reach = drain_ref[1:2, :]
    digits = jnp.concatenate([reach // 16, reach % 16, jnp.zeros((6, reaches), jnp.int32)], axis=0)
    found = jnp.dot(digits.astype(F32).astype(BF16), send_table, preferred_element_type=F32)
    targets = 16.0 * found[0:1] + found[1:2]
    lay_out(outgoing_ref, choose(route(runoff, coefficients), send_table))
    lay_out(outgoing_ref, jnp.broadcast_to(targets, (ID_ROWS, basins * capacity)), days)


def first_unpack_body(received_ref, arrive_ref, recv_table_ref):
    days, reaches = arrive_ref.shape
    targets = take_in(received_ref, days, 1)
    recv_table = one_hot(as_column(targets), reaches)
    recv_table_ref[...] = recv_table
    arrive_ref[...] = choose(take_in(received_ref, 0, days), recv_table)


def unpack_body(received_ref, recv_table_ref, arrive_ref):
    arrive_ref[...] = choose(take_in(received_ref, 0, arrive_ref.shape[0]), recv_table_ref[...])


def coefficient_rows(ref):
    return tuple(ref[row : row + 1, :] for row in range(3))


def pack_body(*refs):
    runoff_ref, coefficients_ref, send_table_ref, *arrive_refs, outgoing_ref = refs
    inflow = runoff_ref[...]
    for ref in arrive_refs:
        inflow = inflow + ref[...]
    routed = route(inflow, coefficient_rows(coefficients_ref))
    lay_out(outgoing_ref, choose(routed, send_table_ref[...]))


def last_body(*refs):
    runoff_ref, coefficients_ref, *arrive_refs, out_ref = refs
    inflow = runoff_ref[...]
    for ref in arrive_refs:
        inflow = inflow + ref[...]
    out_ref[...] = route(inflow, coefficient_rows(coefficients_ref))


def per_device(
    forcings, w_input, w_recur, gate_bias, w_runoff, travel_time, weight_x, drain_basin, drain_reach
):
    basins = lax.axis_size("basin")
    groups = lax.axis_size("order")
    days, channels, reaches = forcings.shape
    units = w_recur.shape[1]
    capacity = 2 * reaches // basins
    slots = basins * capacity
    split = capacity % 128 == 0

    def payload(rows):
        return jax.ShapeDtypeStruct((basins, rows, capacity) if split else (rows, slots), F32)

    def series():
        return jax.ShapeDtypeStruct((days, reaches), F32)

    def exchange(outgoing):
        if split:
            return lax.all_to_all(outgoing, "basin", split_axis=0, concat_axis=0, tiled=True)
        outgoing = outgoing.reshape(-1, basins, capacity)
        received = lax.all_to_all(outgoing, "basin", split_axis=1, concat_axis=1, tiled=True)
        return received.reshape(-1, slots)

    params = jnp.stack([travel_time, weight_x])
    drain = jnp.stack([drain_basin[:, 0], drain_reach[:, 0]])
    runoff, coefficients, send_table, outgoing = call(
        functools.partial(first_body, days=days, basins=basins),
        [
            series(),
            jax.ShapeDtypeStruct((3, reaches), F32),
            jax.ShapeDtypeStruct((reaches, slots), BF16),
            payload(days + ID_ROWS),
        ],
        megabytes=24,
        scratch_shapes=[
            pltpu.VMEM((units // channels, 2 * units, 4 * units), BF16),
            pltpu.VMEM((reaches, units), F32),
        ],
    )(
        forcings.reshape(days * channels, reaches),
        w_input,
        w_recur,
        gate_bias[None, :],
        w_runoff[None, :],
        params,
        drain,
    )
    arrivals = []
    recv_table = None
    for section in range(groups - 1):
        if section > 0:
            outgoing = call(pack_body, payload(days))(runoff, coefficients, send_table, *arrivals)
        received = exchange(outgoing)
        if section == 0:
            arrive, recv_table = call(
                first_unpack_body, [series(), jax.ShapeDtypeStruct((slots, reaches), BF16)]
            )(received)
        else:
            arrive = call(unpack_body, series())(received, recv_table)
        pairs = [
            (section * basins + basin, (section + 1) * basins + basin) for basin in range(basins)
        ]
        arrivals.append(lax.ppermute(arrive, ("order", "basin"), pairs))
    return call(last_body, series())(runoff, coefficients, *arrivals)


def solution(mesh):
    return jax.shard_map(
        per_device,
        mesh=mesh,
        in_specs=(
            P(None, None, ("order", "basin")),
            P(),
            P(),
            P(),
            P(),
            P(("order", "basin")),
            P(("order", "basin")),
            P(("order", "basin"), None),
            P(("order", "basin"), None),
        ),
        out_specs=P(None, ("order", "basin")),
        check_vma=False,
    )
```

```python
import functools

import jax
import jax.numpy as jnp
from jax import lax
from jax.experimental import pallas as pl
from jax.experimental.pallas import tpu as pltpu
from jax.sharding import PartitionSpec as P

F32 = jnp.float32
BF16 = jnp.bfloat16
ID_ROWS = 8
CHUNK = 256


def vmem():
    return pl.BlockSpec(memory_space=pltpu.VMEM)


def call(body, out_shape, megabytes=8, **more):
    return pl.pallas_call(
        body,
        out_shape=out_shape,
        out_specs=jax.tree.map(lambda _: vmem(), out_shape),
        compiler_params=pltpu.CompilerParams(vmem_limit_bytes=megabytes << 20),
        **more,
    )


def delayed(series, days):
    return jnp.concatenate(
        [jnp.zeros((days, series.shape[1]), series.dtype), series[: series.shape[0] - days]], axis=0
    )


def routing_coefficients(travel_time, weight_x):
    held = travel_time * (1.0 - weight_x)
    denominator = held + 0.5
    coeff_first = (0.5 - travel_time * weight_x) / denominator
    coeff_second = (0.5 + travel_time * weight_x) / denominator
    recession = (held - 0.5) / denominator
    return coeff_first, coeff_first * recession + coeff_second, recession


def route(inflow, coefficients):
    first, later, recession = coefficients
    stored, power, reach = inflow, recession, 1
    while reach < inflow.shape[0]:
        stored = stored + power * delayed(stored, reach)
        power, reach = power * power, 2 * reach
    return first * inflow + later * delayed(stored, 1)


def in_halves(values):
    high = values.astype(BF16)
    return jnp.concatenate([high, (values - high.astype(F32)).astype(BF16)], axis=0)


def choose(values, table):
    both = jnp.dot(in_halves(values), table, preferred_element_type=F32)
    return both[: values.shape[0]] + both[values.shape[0] :]


def as_column(row):
    return jnp.transpose(jnp.broadcast_to(row, (8, row.shape[1])))[:, :1]


def one_hot(index_column, width):
    lanes = lax.broadcasted_iota(jnp.int32, (index_column.shape[0], width), 1).astype(F32)
    return jnp.where(index_column == lanes, 1.0, 0.0).astype(BF16)


def lay_out(ref, rows, first_row=0):
    count = rows.shape[0]
    if len(ref.shape) == 2:
        ref[first_row : first_row + count, :] = rows
    else:
        capacity = ref.shape[2]
        for basin in range(ref.shape[0]):
            ref[basin, first_row : first_row + count, :] = rows[
                :, basin * capacity : (basin + 1) * capacity
            ]


def take_in(ref, first_row, count):
    if len(ref.shape) == 2:
        return ref[first_row : first_row + count, :]
    return jnp.concatenate(
        [ref[basin, first_row : first_row + count, :] for basin in range(ref.shape[0])], axis=1
    )


def send_slots(drain_to, basins, capacity):
    reaches = drain_to.shape[1]
    basin_rows = max(basins, 8)
    member = (lax.broadcasted_iota(jnp.int32, (basin_rows, reaches), 0) == drain_to).astype(F32)
    before = lax.broadcasted_iota(jnp.int32, (reaches, reaches), 0)
    after = lax.broadcasted_iota(jnp.int32, (reaches, reaches), 1)
    upper = jnp.where(before < after, 1.0, 0.0).astype(BF16)
    earlier = jnp.dot(member.astype(BF16), upper, preferred_element_type=F32)
    rank = jnp.sum(member * earlier, axis=0, keepdims=True)
    return drain_to.astype(F32) * capacity + rank


def first_body(
    forcings_hbm,
    w_input_hbm,
    w_recur_hbm,
    gate_bias_hbm,
    w_runoff_hbm,
    travel_hbm,
    weight_hbm,
    drain_basin_hbm,
    drain_reach_hbm,
    runoff_ref,
    coefficients_ref,
    send_table_ref,
    targets_ref,
    forcings_ref,
    w_input_ref,
    w_recur_ref,
    gate_bias_ref,
    w_runoff_ref,
    travel_ref,
    weight_ref,
    drain_basin_ref,
    drain_reach_ref,
    weights,
    sums,
    arrived,
    *,
    days,
    basins,
):
    loads = [
        pltpu.make_async_copy(source, target, arrived.at[number])
        for number, (source, target) in enumerate(
            [
                (w_recur_hbm, w_recur_ref),
                (w_input_hbm, w_input_ref),
                (gate_bias_hbm, gate_bias_ref),
                (w_runoff_hbm, w_runoff_ref),
                (travel_hbm, travel_ref),
                (weight_hbm, weight_ref),
                (drain_basin_hbm, drain_basin_ref),
                (drain_reach_hbm, drain_reach_ref),
                (forcings_hbm, forcings_ref),
            ]
        )
    ]
    for load in loads:
        load.start()
    reaches = forcings_ref.shape[1]
    channels = forcings_ref.shape[0] // days
    units = w_recur_ref.shape[1]
    gates = 4 * units
    per_block = units // channels
    capacity = 2 * reaches // basins
    sums[...] = jnp.zeros_like(sums)
    for day in range(per_block):
        weights[day, units:, :] = jnp.zeros((units, gates), BF16)
    for load in loads[:-1]:
        load.wait()

    gate_lane = lax.broadcasted_iota(jnp.int32, (1, gates), 1)
    is_candidate = (gate_lane >= 2 * units) & (gate_lane < 3 * units)
    scale = jnp.where(is_candidate, 1.0, 0.5)
    recur = (jnp.transpose(w_recur_ref[...].astype(F32)) * (0.5 * scale)).astype(BF16)
    inputs = (w_input_ref[...].astype(F32) * scale).astype(BF16)
    bias = gate_bias_ref[...] * scale
    readout = 0.5 * w_runoff_ref[...]
    for day in range(per_block):
        weights[day, :units, :] = recur
        weights[day, units + day * channels : units + (day + 1) * channels, :] = inputs
    chunk = min(CHUNK, reaches)
    chunks = reaches // chunk
    lane = lax.broadcasted_iota(jnp.int32, (chunk, units), 1)

    coefficients = routing_coefficients(travel_ref[...], weight_ref[...])
    for row in range(3):
        coefficients_ref[row : row + 1, :] = coefficients[row]
    slots = send_slots(drain_basin_ref[...], basins, capacity)
    send_table = one_hot(as_column(slots), basins * capacity)
    send_table_ref[...] = send_table
    reach = drain_reach_ref[...]
    digits = jnp.concatenate([reach // 16, reach % 16, jnp.zeros((6, reaches), jnp.int32)], axis=0)
    found = jnp.dot(digits.astype(F32).astype(BF16), send_table, preferred_element_type=F32)
    targets_ref[...] = jnp.broadcast_to(16.0 * found[0:1] + found[1:2], targets_ref.shape)
    loads[-1].wait()

    def block_of_days(block, state):
        rows = pl.ds(pl.multiple_of(block * units, units), units)
        forced = jnp.transpose(forcings_ref[rows, :].astype(F32)).astype(BF16)
        state = list(state)
        for day in range(per_block):
            for part in range(chunks):
                hidden, memory = state[part]
                span = slice(part * chunk, (part + 1) * chunk)
                gate_sums = bias + jnp.dot(
                    jnp.concatenate([hidden, forced[span]], axis=1),
                    weights[day],
                    preferred_element_type=F32,
                )
                ingate = jnp.tanh(gate_sums[:, :units])
                forget = jnp.tanh(gate_sums[:, units : 2 * units])
                candidate = jnp.tanh(gate_sums[:, 2 * units : 3 * units])
                outgate = jnp.tanh(gate_sums[:, 3 * units :])
                memory = 0.5 * ((forget * memory + memory) + (ingate * candidate + candidate))
                squashed = jnp.tanh(memory)
                hidden = (outgate * squashed + squashed).astype(BF16)
                drained = jnp.sum(hidden.astype(F32) * readout, axis=1, keepdims=True)
                sums[span, :] = jnp.where(lane == block * per_block + day, drained, sums[span, :])
                state[part] = (hidden, memory)
        return tuple(state)

    state = tuple(
        (jnp.zeros((chunk, units), BF16), jnp.zeros((chunk, units), F32)) for _ in range(chunks)
    )
    lax.fori_loop(0, days // per_block, block_of_days, state)
    pre = jnp.transpose(sums[...])[:days]
    runoff = jnp.maximum(pre, 0.0) + jnp.log1p(jnp.exp(-jnp.abs(pre)))
    runoff_ref[...] = runoff


def pack_body(runoff_ref, coefficients_ref, send_table_ref, targets_ref, arrive_ref, outgoing_ref):
    routed = route(runoff_ref[...] + arrive_ref[...], coefficient_rows(coefficients_ref))
    lay_out(outgoing_ref, choose(routed, send_table_ref[...]))
    lay_out(outgoing_ref, targets_ref[...], routed.shape[0])


def unpack_body(received_ref, arrive_ref):
    days, reaches = arrive_ref.shape
    recv_table = one_hot(as_column(take_in(received_ref, days, 1)), reaches)
    arrive_ref[...] = choose(take_in(received_ref, 0, days), recv_table)


def last_body(runoff_ref, coefficients_ref, arrive_ref, out_ref):
    out_ref[...] = route(
        runoff_ref[...] + arrive_ref[...], coefficient_rows(coefficients_ref)
    )


def coefficient_rows(ref):
    return tuple(ref[row : row + 1, :] for row in range(3))


def handed_on(passed, section, groups, basins):
    turned = [(2 * section + 1 - group) % groups for group in range(groups)]
    pairs = [
        (group * basins + basin, turned[group] * basins + basin)
        for group in range(groups)
        for basin in range(basins)
    ]
    received = lax.ppermute(passed, ("order", "basin"), pairs)
    return jnp.where(lax.axis_index("order") == section + 1, received, 0.0)


def per_device(
    forcings, w_input, w_recur, gate_bias, w_runoff, travel_time, weight_x, drain_basin, drain_reach
):
    basins = lax.axis_size("basin")
    groups = lax.axis_size("order")
    days, channels, reaches = forcings.shape
    units = w_recur.shape[1]
    capacity = 2 * reaches // basins
    slots = basins * capacity
    split = capacity % 128 == 0

    def payload(rows):
        return jax.ShapeDtypeStruct((basins, rows, capacity) if split else (rows, slots), F32)

    def series():
        return jax.ShapeDtypeStruct((days, reaches), F32)

    def exchange(outgoing):
        if split:
            return lax.all_to_all(outgoing, "basin", split_axis=0, concat_axis=0, tiled=True)
        outgoing = outgoing.reshape(-1, basins, capacity)
        received = lax.all_to_all(outgoing, "basin", split_axis=1, concat_axis=1, tiled=True)
        return received.reshape(-1, slots)

    def row(values):
        return values.reshape(1, -1)

    operands = (
        forcings.reshape(days * channels, reaches),
        w_input.T,
        w_recur,
        row(gate_bias),
        row(w_runoff),
        row(travel_time),
        row(weight_x),
        row(drain_basin),
        row(drain_reach),
    )
    runoff, coefficients, send_table, targets = call(
        functools.partial(first_body, days=days, basins=basins),
        [
            series(),
            jax.ShapeDtypeStruct((3, reaches), F32),
            jax.ShapeDtypeStruct((reaches, slots), BF16),
            jax.ShapeDtypeStruct((ID_ROWS, slots), F32),
        ],
        megabytes=56,
        in_specs=[pl.BlockSpec(memory_space=pltpu.HBM) for _ in operands],
        scratch_shapes=[pltpu.VMEM(array.shape, array.dtype) for array in operands]
        + [
            pltpu.VMEM((units // channels, 2 * units, 4 * units), BF16),
            pltpu.VMEM((reaches, units), F32),
            pltpu.SemaphoreType.DMA((len(operands),)),
        ],
    )(*operands)

    def send(arrive):
        outgoing = call(pack_body, payload(days + ID_ROWS))(
            runoff, coefficients, send_table, targets, arrive
        )
        return call(unpack_body, series())(exchange(outgoing))

    def stay(arrive):
        return jnp.zeros_like(arrive)

    group = lax.axis_index("order")
    arrive = jnp.zeros((days, reaches), F32)
    for section in range(groups - 1):
        passed = lax.cond(group == section, send, stay, arrive)
        arrive = arrive + handed_on(passed, section, groups, basins)
    return call(last_body, series())(runoff, coefficients, arrive)


def solution(mesh):
    return jax.shard_map(
        per_device,
        mesh=mesh,
        in_specs=(
            P(None, None, ("order", "basin")),
            P(),
            P(),
            P(),
            P(),
            P(("order", "basin")),
            P(("order", "basin")),
            P(("order", "basin"), None),
            P(("order", "basin"), None),
        ),
        out_specs=P(None, ("order", "basin")),
        check_vma=False,
    )
```

```python
import functools

import jax
import jax.numpy as jnp
from jax import lax
from jax.experimental import pallas as pl
from jax.experimental.pallas import tpu as pltpu
from jax.sharding import PartitionSpec as P

F32 = jnp.float32
BF16 = jnp.bfloat16
ID_ROWS = 8
TABLE_ROWS = 16
INFO_ROWS = 8
CHUNK = 256


def vmem():
    return pl.BlockSpec(memory_space=pltpu.VMEM)


def call(body, out_shape, megabytes=8, **more):
    return pl.pallas_call(
        body,
        out_shape=out_shape,
        out_specs=jax.tree.map(lambda _: vmem(), out_shape),
        compiler_params=pltpu.CompilerParams(vmem_limit_bytes=megabytes << 20),
        **more,
    )


def delayed(series, days):
    return jnp.concatenate(
        [jnp.zeros((days, series.shape[1]), series.dtype), series[: series.shape[0] - days]], axis=0
    )


def routing_coefficients(travel_time, weight_x):
    held = travel_time * (1.0 - weight_x)
    denominator = held + 0.5
    coeff_first = (0.5 - travel_time * weight_x) / denominator
    coeff_second = (0.5 + travel_time * weight_x) / denominator
    recession = (held - 0.5) / denominator
    return coeff_first, coeff_first * recession + coeff_second, recession


def route(inflow, coefficients):
    first, later, recession = coefficients
    stored, power, reach = inflow, recession, 1
    while reach < inflow.shape[0]:
        stored = stored + power * delayed(stored, reach)
        power, reach = power * power, 2 * reach
    return first * inflow + later * delayed(stored, 1)


def in_halves(values):
    high = values.astype(BF16)
    return jnp.concatenate([high, (values - high.astype(F32)).astype(BF16)], axis=0)


def choose(values, table):
    both = jnp.dot(in_halves(values), table, preferred_element_type=F32)
    return both[: values.shape[0]] + both[values.shape[0] :]


def as_column(row):
    return jnp.transpose(jnp.broadcast_to(row, (8, row.shape[1])))[:, :1]


def one_hot(index_column, width):
    lanes = lax.broadcasted_iota(jnp.int32, (index_column.shape[0], width), 1).astype(F32)
    return jnp.where(index_column == lanes, 1.0, 0.0).astype(BF16)


def lay_out(ref, rows, first_row=0):
    count = rows.shape[0]
    if len(ref.shape) == 2:
        ref[first_row : first_row + count, :] = rows
    else:
        capacity = ref.shape[2]
        for basin in range(ref.shape[0]):
            ref[basin, first_row : first_row + count, :] = rows[
                :, basin * capacity : (basin + 1) * capacity
            ]


def take_in(ref, first_row, count):
    if len(ref.shape) == 2:
        return ref[first_row : first_row + count, :]
    return jnp.concatenate(
        [ref[basin, first_row : first_row + count, :] for basin in range(ref.shape[0])], axis=1
    )


def send_slots(drain_to, basins, capacity):
    reaches = drain_to.shape[1]
    basin_rows = max(basins, 8)
    member = (lax.broadcasted_iota(jnp.int32, (basin_rows, reaches), 0) == drain_to).astype(F32)
    before = lax.broadcasted_iota(jnp.int32, (reaches, reaches), 0)
    after = lax.broadcasted_iota(jnp.int32, (reaches, reaches), 1)
    upper = jnp.where(before < after, 1.0, 0.0).astype(BF16)
    earlier = jnp.dot(member.astype(BF16), upper, preferred_element_type=F32)
    rank = jnp.sum(member * earlier, axis=0, keepdims=True)
    return drain_to.astype(F32) * capacity + rank


def first_body(
    forcings_hbm,
    w_input_hbm,
    w_recur_hbm,
    gate_bias_hbm,
    w_runoff_hbm,
    travel_hbm,
    weight_hbm,
    drain_basin_hbm,
    drain_reach_hbm,
    runoff_ref,
    info_ref,
    told_ref,
    blank_ready_ref,
    blank_table_ref,
    send_table_ref,
    targets_ref,
    outgoing_ref,
    forcings_ref,
    w_input_ref,
    w_recur_ref,
    gate_bias_ref,
    w_runoff_ref,
    travel_ref,
    weight_ref,
    drain_basin_ref,
    drain_reach_ref,
    weights,
    sums,
    arrived,
    *,
    days,
    basins,
):
    loads = [
        pltpu.make_async_copy(source, target, arrived.at[number])
        for number, (source, target) in enumerate(
            [
                (w_recur_hbm, w_recur_ref),
                (w_input_hbm, w_input_ref),
                (gate_bias_hbm, gate_bias_ref),
                (w_runoff_hbm, w_runoff_ref),
                (travel_hbm, travel_ref),
                (weight_hbm, weight_ref),
                (drain_basin_hbm, drain_basin_ref),
                (drain_reach_hbm, drain_reach_ref),
                (forcings_hbm, forcings_ref),
            ]
        )
    ]
    for load in loads:
        load.start()
    reaches = forcings_ref.shape[1]
    channels = forcings_ref.shape[0] // days
    units = w_recur_ref.shape[1]
    gates = 4 * units
    per_block = units // channels
    capacity = 2 * reaches // basins
    sums[...] = jnp.zeros_like(sums)
    for day in range(per_block):
        weights[day, units:, :] = jnp.zeros((units, gates), BF16)
    for load in loads[:-1]:
        load.wait()

    gate_lane = lax.broadcasted_iota(jnp.int32, (1, gates), 1)
    is_candidate = (gate_lane >= 2 * units) & (gate_lane < 3 * units)
    scale = jnp.where(is_candidate, 1.0, 0.5)
    recur = (jnp.transpose(w_recur_ref[...].astype(F32)) * (0.5 * scale)).astype(BF16)
    inputs = (w_input_ref[...].astype(F32) * scale).astype(BF16)
    bias = gate_bias_ref[...] * scale
    readout = 0.5 * w_runoff_ref[...]
    for day in range(per_block):
        weights[day, :units, :] = recur
        weights[day, units + day * channels : units + (day + 1) * channels, :] = inputs
    chunk = min(CHUNK, reaches)
    chunks = reaches // chunk
    lane = lax.broadcasted_iota(jnp.int32, (chunk, units), 1)

    coefficients = routing_coefficients(travel_ref[...], weight_ref[...])
    reach = drain_reach_ref[...]
    known = (drain_basin_ref[...].astype(F32), reach.astype(F32)) + coefficients
    for row, values in enumerate(known):
        info_ref[row : row + 1, :] = values
    info_ref[len(known) :, :] = jnp.zeros((INFO_ROWS - len(known), reaches), F32)
    blank_ready_ref[...] = jnp.zeros_like(blank_ready_ref)
    blank_table_ref[...] = jnp.zeros_like(blank_table_ref)
    slots = send_slots(drain_basin_ref[...], basins, capacity)
    send_table = one_hot(as_column(slots), basins * capacity)
    send_table_ref[...] = send_table
    digits = jnp.concatenate([reach // 16, reach % 16, jnp.zeros((6, reaches), jnp.int32)], axis=0)
    found = jnp.dot(digits.astype(F32).astype(BF16), send_table, preferred_element_type=F32)
    targets_ref[...] = jnp.broadcast_to(16.0 * found[0:1] + found[1:2], targets_ref.shape)
    loads[-1].wait()

    def block_of_days(block, state):
        rows = pl.ds(pl.multiple_of(block * units, units), units)
        forced = jnp.transpose(forcings_ref[rows, :].astype(F32)).astype(BF16)
        state = list(state)
        for day in range(per_block):
            for part in range(chunks):
                hidden, memory = state[part]
                span = slice(part * chunk, (part + 1) * chunk)
                gate_sums = bias + jnp.dot(
                    jnp.concatenate([hidden, forced[span]], axis=1),
                    weights[day],
                    preferred_element_type=F32,
                )
                ingate = jnp.tanh(gate_sums[:, :units])
                forget = jnp.tanh(gate_sums[:, units : 2 * units])
                candidate = jnp.tanh(gate_sums[:, 2 * units : 3 * units])
                outgate = jnp.tanh(gate_sums[:, 3 * units :])
                memory = 0.5 * ((forget * memory + memory) + (ingate * candidate + candidate))
                squashed = jnp.tanh(memory)
                hidden = (outgate * squashed + squashed).astype(BF16)
                drained = jnp.sum(hidden.astype(F32) * readout, axis=1, keepdims=True)
                sums[span, :] = jnp.where(lane == block * per_block + day, drained, sums[span, :])
                state[part] = (hidden, memory)
        return tuple(state)

    state = tuple(
        (jnp.zeros((chunk, units), BF16), jnp.zeros((chunk, units), F32)) for _ in range(chunks)
    )
    lax.fori_loop(0, days // per_block, block_of_days, state)
    pre = jnp.transpose(sums[...])[:days]
    runoff = jnp.maximum(pre, 0.0) + jnp.log1p(jnp.exp(-jnp.abs(pre)))
    runoff_ref[...] = runoff
    routed = route(runoff, coefficients)
    told_ref[:days] = routed
    told_ref[days:] = info_ref[...]
    lay_out(outgoing_ref, choose(routed, send_table_ref[...]))
    lay_out(outgoing_ref, targets_ref[...], days)


def info_coefficients(ref):
    return tuple(ref[row : row + 1, :] for row in range(2, 5))


def pack_body(runoff_ref, info_ref, send_table_ref, targets_ref, arrive_ref, outgoing_ref):
    routed = route(runoff_ref[...] + arrive_ref[...], info_coefficients(info_ref))
    lay_out(outgoing_ref, choose(routed, send_table_ref[...]))
    lay_out(outgoing_ref, targets_ref[...], routed.shape[0])


def unpack_body(received_ref, arrive_ref):
    days, reaches = arrive_ref.shape
    recv_table = one_hot(as_column(take_in(received_ref, days, 1)), reaches)
    arrive_ref[...] = choose(take_in(received_ref, 0, days), recv_table)


def pass_body(runoff_ref, info_ref, arrive_ref, out_ref):
    days = runoff_ref.shape[0]
    route_body(runoff_ref, info_ref, arrive_ref, out_ref.at[:days])
    out_ref[days:] = info_ref[...]


def route_body(runoff_ref, info_ref, arrive_ref, out_ref):
    out_ref[...] = route(runoff_ref[...] + arrive_ref[...], info_coefficients(info_ref))


def in_thirds(values):
    high = values.astype(BF16)
    rest = values - high.astype(F32)
    middle = rest.astype(BF16)
    return [high, middle, (rest - middle.astype(F32)).astype(BF16)]


def spread_body(told_ref, out_ref):
    for basin in range(out_ref.shape[0]):
        out_ref[basin] = told_ref[told_ref.shape[0] - INFO_ROWS :, :]


def info_table(tables_ref):
    pieces = []
    for basin in range(tables_ref.shape[0]):
        reach = tables_ref[basin, 1:2, :].astype(jnp.int32)
        rows = [tables_ref[basin, 0:1, :], (reach // 16).astype(F32), (reach % 16).astype(F32)]
        for row in range(2, 5):
            rows += [third.astype(F32) for third in in_thirds(tables_ref[basin, row : row + 1, :])]
        rows.append(jnp.zeros((TABLE_ROWS - len(rows), reach.shape[1]), F32))
        pieces.append(jnp.concatenate(rows, axis=0).astype(BF16))
    return jnp.concatenate(pieces, axis=0)


def looked_up(table, from_basin, from_reach):
    reaches = table.shape[1]
    sublanes = lax.broadcasted_iota(jnp.int32, (reaches, reaches), 0).astype(F32)
    pick = jnp.where(sublanes == from_reach, 1.0, 0.0).astype(BF16)
    picked = jnp.dot(table, pick, preferred_element_type=F32)
    found = jnp.zeros((TABLE_ROWS, reaches), F32)
    for basin in range(table.shape[0] // TABLE_ROWS):
        here = from_basin == float(basin)
        found = found + jnp.where(here, picked[basin * TABLE_ROWS : (basin + 1) * TABLE_ROWS], 0.0)
    coefficients = tuple(
        (found[row : row + 1] + found[row + 1 : row + 2]) + found[row + 2 : row + 3]
        for row in (3, 6, 9)
    )
    return found[0:1], 16.0 * found[1:2] + found[2:3], coefficients


def by_target(values, to_basin, to_reach, basins):
    days, reaches = values.shape
    halves = in_halves(values).astype(F32)
    parts = [
        jnp.where(to_basin == float(basin), halves, 0.0).astype(BF16) for basin in range(basins)
    ]
    table = one_hot(as_column(to_reach), reaches)
    sums = jnp.dot(jnp.concatenate(parts, axis=0), table, preferred_element_type=F32)
    return [
        sums[first : first + days] + sums[first + days : first + 2 * days]
        for first in range(0, 2 * basins * days, 2 * days)
    ]


def prepare_body(before_ref, tables_ref, ready_ref, table_ref):
    basins, days, _ = ready_ref.shape
    table_ref[...] = info_table(tables_ref)
    to_basin, to_reach = before_ref[days : days + 1, :], before_ref[days + 1 : days + 2, :]
    for basin, sums in enumerate(by_target(before_ref[:days, :], to_basin, to_reach, basins)):
        ready_ref[basin] = sums


def pack_beyond_body(passed_ref, ready_ref, table_ref, outgoing_ref):
    basins, days, _ = outgoing_ref.shape
    to_basin, to_reach, coefficients = looked_up(
        table_ref[...], passed_ref[days : days + 1, :], passed_ref[days + 1 : days + 2, :]
    )
    routed = route(passed_ref[:days, :], coefficients)
    for basin, sums in enumerate(by_target(routed, to_basin, to_reach, basins)):
        outgoing_ref[basin] = ready_ref[basin] + sums


def add_up_body(received_ref, arrive_ref):
    total = received_ref[0]
    for basin in range(1, received_ref.shape[0]):
        total = total + received_ref[basin]
    arrive_ref[...] = total


def per_device(
    forcings, w_input, w_recur, gate_bias, w_runoff, travel_time, weight_x, drain_basin, drain_reach
):
    basins = lax.axis_size("basin")
    groups = lax.axis_size("order")
    days, channels, reaches = forcings.shape
    units = w_recur.shape[1]
    capacity = 2 * reaches // basins
    slots = basins * capacity
    split = capacity % 128 == 0

    def series():
        return jax.ShapeDtypeStruct((days, reaches), F32)

    def swap(outgoing):
        return lax.all_to_all(outgoing, "basin", split_axis=0, concat_axis=0, tiled=True)

    def exchange(outgoing):
        if split:
            return swap(outgoing)
        outgoing = outgoing.reshape(-1, basins, capacity)
        received = lax.all_to_all(outgoing, "basin", split_axis=1, concat_axis=1, tiled=True)
        return received.reshape(-1, slots)

    def row(values):
        return values.reshape(1, -1)

    operands = (
        forcings.reshape(days * channels, reaches),
        w_input.T,
        w_recur,
        row(gate_bias),
        row(w_runoff),
        row(travel_time),
        row(weight_x),
        row(drain_basin),
        row(drain_reach),
    )
    info_shape = jax.ShapeDtypeStruct((INFO_ROWS, reaches), F32)
    told_shape = jax.ShapeDtypeStruct((days + INFO_ROWS, reaches), F32)
    ready_shape = jax.ShapeDtypeStruct((basins, days, reaches), F32)
    table_shape = jax.ShapeDtypeStruct((basins * TABLE_ROWS, reaches), BF16)
    payload_shape = jax.ShapeDtypeStruct(
        (basins, days + ID_ROWS, capacity) if split else (days + ID_ROWS, slots), F32
    )
    runoff, info, told, ready, table, send_table, targets, outgoing = call(
        functools.partial(first_body, days=days, basins=basins),
        [
            series(),
            info_shape,
            told_shape,
            ready_shape,
            table_shape,
            jax.ShapeDtypeStruct((reaches, slots), BF16),
            jax.ShapeDtypeStruct((ID_ROWS, slots), F32),
            payload_shape,
        ],
        megabytes=56,
        in_specs=[pl.BlockSpec(memory_space=pltpu.HBM) for _ in operands],
        scratch_shapes=[pltpu.VMEM(array.shape, array.dtype) for array in operands]
        + [
            pltpu.VMEM((units // channels, 2 * units, 4 * units), BF16),
            pltpu.VMEM((reaches, units), F32),
            pltpu.SemaphoreType.DMA((len(operands),)),
        ],
    )(*operands)

    group = lax.axis_index("order")
    later = range(1, groups // 2)

    def moved(block, routes):
        pairs = [
            (source * basins + basin, target * basins + basin)
            for source, target in routes
            for basin in range(basins)
        ]
        return lax.ppermute(block, ("order", "basin"), pairs)

    neighbours = [(place, place ^ 1) for place in range(groups)]
    two_down = [(place, (place + 2) % groups) for place in range(groups)]

    def nothing(*_):
        return jnp.zeros((days, reaches), F32)

    def learn(told, ready, table):
        before = moved(told, neighbours)

        def prepare(before, ready, table):
            spread = jax.ShapeDtypeStruct((basins, INFO_ROWS, reaches), F32)
            tables = swap(call(spread_body, spread)(before))
            return tuple(call(prepare_body, [ready_shape, table_shape], 24)(before, tables))

        return lax.cond(
            group % 2 == 1,
            prepare,
            lambda before, ready, table: (ready, table),
            before,
            ready,
            table,
        )

    ready, table = lax.cond(
        group > 1, learn, lambda told, ready, table: (ready, table), told, ready, table
    )
    outgoing, ready, table = lax.optimization_barrier((outgoing, ready, table))

    def deliver(outgoing):
        return call(unpack_body, series())(exchange(outgoing))

    arrive = moved(lax.cond(group == 0, deliver, nothing, outgoing), neighbours)
    arrive = jnp.where(group == 1, arrive, 0.0)
    for pair in later:
        above, between, below = 2 * pair - 1, 2 * pair, 2 * pair + 1
        passed = moved(call(pass_body, told_shape)(runoff, info, arrive), two_down)
        delivered = lax.cond(
            group == above,
            lambda arrive: deliver(
                call(pack_body, payload_shape)(runoff, info, send_table, targets, arrive)
            ),
            nothing,
            arrive,
        )
        passed, delivered = lax.optimization_barrier((passed, delivered))
        received = lax.cond(
            group == below,
            lambda passed, _: call(add_up_body, series())(
                swap(call(pack_beyond_body, ready_shape, 24)(passed, ready, table))
            ),
            lambda _, delivered: delivered,
            passed,
            delivered,
        )
        received = lax.cond(
            (group == above) | (group == between),
            lambda received: moved(received, [(above, between)]),
            lambda received: received,
            received,
        )
        arrive = arrive + jnp.where(group == above, 0.0, received)
    return call(route_body, series())(runoff, info, arrive)


def solution(mesh):
    return jax.shard_map(
        per_device,
        mesh=mesh,
        in_specs=(
            P(None, None, ("order", "basin")),
            P(),
            P(),
            P(),
            P(),
            P(("order", "basin")),
            P(("order", "basin")),
            P(("order", "basin"), None),
            P(("order", "basin"), None),
        ),
        out_specs=P(None, ("order", "basin")),
        check_vma=False,
    )
```

```python
import functools

import jax
import jax.numpy as jnp
from jax import lax
from jax.experimental import pallas as pl
from jax.experimental.pallas import tpu as pltpu
from jax.sharding import PartitionSpec as P

F32 = jnp.float32
BF16 = jnp.bfloat16
ID_ROWS = 8
TABLE_ROWS = 16
KNOWN = 5
INFO_ROWS = 8
CHUNK = 512


def vmem():
    return pl.BlockSpec(memory_space=pltpu.VMEM)


def call(body, out_shape, megabytes=8, **more):
    return pl.pallas_call(
        body,
        out_shape=out_shape,
        out_specs=jax.tree.map(lambda _: vmem(), out_shape),
        compiler_params=pltpu.CompilerParams(vmem_limit_bytes=megabytes << 20),
        **more,
    )


def delayed(series, days):
    return jnp.concatenate(
        [jnp.zeros((days, series.shape[1]), series.dtype), series[: series.shape[0] - days]], axis=0
    )


def routing_coefficients(travel_time, weight_x):
    held = travel_time * (1.0 - weight_x)
    denominator = held + 0.5
    coeff_first = (0.5 - travel_time * weight_x) / denominator
    coeff_second = (0.5 + travel_time * weight_x) / denominator
    recession = (held - 0.5) / denominator
    return coeff_first, coeff_first * recession + coeff_second, recession


def route(inflow, coefficients):
    first, later, recession = coefficients
    stored, power, reach = inflow, recession, 1
    while reach < inflow.shape[0]:
        stored = stored + power * delayed(stored, reach)
        power, reach = power * power, 2 * reach
    return first * inflow + later * delayed(stored, 1)


def in_halves(values):
    high = values.astype(BF16)
    return jnp.concatenate([high, (values - high.astype(F32)).astype(BF16)], axis=0)


def choose(values, table):
    both = jnp.dot(in_halves(values), table, preferred_element_type=F32)
    return both[: values.shape[0]] + both[values.shape[0] :]


def as_column(row):
    return jnp.transpose(jnp.broadcast_to(row, (8, row.shape[1])))[:, :1]


def one_hot(index_column, width):
    lanes = lax.broadcasted_iota(jnp.int32, (index_column.shape[0], width), 1).astype(F32)
    return jnp.where(index_column == lanes, 1.0, 0.0).astype(BF16)


def lay_out(ref, rows, first_row=0):
    count = rows.shape[0]
    if len(ref.shape) == 2:
        ref[first_row : first_row + count, :] = rows
    else:
        capacity = ref.shape[2]
        for basin in range(ref.shape[0]):
            ref[basin, first_row : first_row + count, :] = rows[
                :, basin * capacity : (basin + 1) * capacity
            ]


def take_in(ref, first_row, count):
    if len(ref.shape) == 2:
        return ref[first_row : first_row + count, :]
    return jnp.concatenate(
        [ref[basin, first_row : first_row + count, :] for basin in range(ref.shape[0])], axis=1
    )


def send_slots(drain_to, basins, capacity):
    reaches = drain_to.shape[1]
    basin_rows = max(basins, 8)
    member = (lax.broadcasted_iota(jnp.int32, (basin_rows, reaches), 0) == drain_to).astype(F32)
    before = lax.broadcasted_iota(jnp.int32, (reaches, reaches), 0)
    after = lax.broadcasted_iota(jnp.int32, (reaches, reaches), 1)
    upper = jnp.where(before < after, 1.0, 0.0).astype(BF16)
    earlier = jnp.dot(member.astype(BF16), upper, preferred_element_type=F32)
    rank = jnp.sum(member * earlier, axis=0, keepdims=True)
    return drain_to.astype(F32) * capacity + rank


def slot_tables(drain_to, reach, basins, capacity):
    send_table = one_hot(as_column(send_slots(drain_to, basins, capacity)), basins * capacity)
    digits = jnp.concatenate(
        [reach // 16, reach % 16, jnp.zeros((6, reach.shape[1]), jnp.int32)], axis=0
    )
    found = jnp.dot(digits.astype(F32).astype(BF16), send_table, preferred_element_type=F32)
    return send_table, jnp.broadcast_to(
        16.0 * found[0:1] + found[1:2], (ID_ROWS, send_table.shape[1])
    )


def known(drain_basin, drain_reach, travel_time, weight_x):
    rows = (drain_basin.astype(F32), drain_reach.astype(F32))
    rows += routing_coefficients(travel_time, weight_x)
    blank = jnp.zeros((INFO_ROWS - len(rows), travel_time.shape[1]), F32)
    return jnp.concatenate([*rows, blank], axis=0)


def coefficients_of(info):
    return tuple(info[row : row + 1, :] for row in range(2, KNOWN))


def first_body(
    forcings_hbm,
    w_input_hbm,
    w_recur_hbm,
    gate_bias_hbm,
    w_runoff_hbm,
    travel_hbm,
    weight_hbm,
    drain_basin_hbm,
    drain_reach_hbm,
    runoff_ref,
    told_ref,
    spread_ref,
    between_ref,
    above_ref,
    ready_ref,
    paths_ref,
    missing_ref,
    absent_ref,
    send_table_ref,
    targets_ref,
    outgoing_ref,
    forcings_ref,
    w_input_ref,
    w_recur_ref,
    gate_bias_ref,
    w_runoff_ref,
    travel_ref,
    weight_ref,
    drain_basin_ref,
    drain_reach_ref,
    weights,
    sums,
    arrived,
    *,
    days,
    basins,
):
    loads = [
        pltpu.make_async_copy(source, target, arrived.at[number])
        for number, (source, target) in enumerate(
            [
                (w_recur_hbm, w_recur_ref),
                (w_input_hbm, w_input_ref),
                (gate_bias_hbm, gate_bias_ref),
                (w_runoff_hbm, w_runoff_ref),
                (travel_hbm, travel_ref),
                (weight_hbm, weight_ref),
                (drain_basin_hbm, drain_basin_ref),
                (drain_reach_hbm, drain_reach_ref),
                (forcings_hbm, forcings_ref),
            ]
        )
    ]
    for load in loads:
        load.start()
    reaches = forcings_ref.shape[1]
    channels = forcings_ref.shape[0] // days
    units = w_recur_ref.shape[1]
    gates = 4 * units
    per_block = units // channels
    capacity = 2 * reaches // basins
    sums[...] = jnp.zeros_like(sums)
    for day in range(per_block):
        weights[day, units:, :] = jnp.zeros((units, gates), BF16)
    for load in loads[:-1]:
        load.wait()

    gate_lane = lax.broadcasted_iota(jnp.int32, (1, gates), 1)
    is_candidate = (gate_lane >= 2 * units) & (gate_lane < 3 * units)
    scale = jnp.where(is_candidate, 1.0, 0.5)
    recur = (jnp.transpose(w_recur_ref[...].astype(F32)) * (0.5 * scale)).astype(BF16)
    inputs = (w_input_ref[...].astype(F32) * scale).astype(BF16)
    bias = gate_bias_ref[...] * scale
    readout = 0.5 * w_runoff_ref[...]
    for day in range(per_block):
        weights[day, :units, :] = recur
        weights[day, units + day * channels : units + (day + 1) * channels, :] = inputs
    chunk = min(CHUNK, reaches)
    chunks = reaches // chunk
    lane = lax.broadcasted_iota(jnp.int32, (chunk, units), 1)

    info = known(drain_basin_ref[...], drain_reach_ref[...], travel_ref[...], weight_ref[...])
    told_ref[days:, :] = info
    for basin in range(basins):
        spread_ref[basin] = info
    send_table, targets = slot_tables(drain_basin_ref[...], drain_reach_ref[...], basins, capacity)
    send_table_ref[...] = send_table
    targets_ref[...] = targets
    for blank_ref in (between_ref, above_ref, ready_ref, paths_ref, missing_ref, absent_ref):
        blank_ref[...] = jnp.zeros_like(blank_ref)
    loads[-1].wait()

    def block_of_days(block, state):
        rows = pl.ds(pl.multiple_of(block * units, units), units)
        forced = jnp.transpose(forcings_ref[rows, :].astype(F32)).astype(BF16)
        state = list(state)
        for day in range(per_block):
            for part in range(chunks):
                hidden, memory = state[part]
                span = slice(part * chunk, (part + 1) * chunk)
                gate_sums = bias + jnp.dot(
                    jnp.concatenate([hidden, forced[span]], axis=1),
                    weights[day],
                    preferred_element_type=F32,
                )
                ingate = jnp.tanh(gate_sums[:, :units])
                forget = jnp.tanh(gate_sums[:, units : 2 * units])
                candidate = jnp.tanh(gate_sums[:, 2 * units : 3 * units])
                outgate = jnp.tanh(gate_sums[:, 3 * units :])
                memory = 0.5 * ((forget * memory + memory) + (ingate * candidate + candidate))
                squashed = jnp.tanh(memory)
                hidden = (outgate * squashed + squashed).astype(BF16)
                drained = jnp.sum(hidden.astype(F32) * readout, axis=1, keepdims=True)
                sums[span, :] = jnp.where(lane == block * per_block + day, drained, sums[span, :])
                state[part] = (hidden, memory)
        return tuple(state)

    state = tuple(
        (jnp.zeros((chunk, units), BF16), jnp.zeros((chunk, units), F32)) for _ in range(chunks)
    )
    lax.fori_loop(0, days // per_block, block_of_days, state, unroll=True)
    pre = jnp.transpose(sums[...])[:days]
    runoff = jnp.maximum(pre, 0.0) + jnp.log1p(jnp.exp(-jnp.abs(pre)))
    runoff_ref[...] = runoff
    routed = route(runoff, coefficients_of(info))
    told_ref[:days, :] = routed
    lay_out(outgoing_ref, choose(routed, send_table_ref[...]))
    lay_out(outgoing_ref, targets_ref[...], days)


def unpack_body(received_ref, *arrive_refs):
    days, reaches = arrive_refs[0].shape
    recv_table = one_hot(as_column(take_in(received_ref, days, 1)), reaches)
    arrive = choose(take_in(received_ref, 0, days), recv_table)
    for arrive_ref in arrive_refs:
        arrive_ref[...] = arrive


def route_body(runoff_ref, told_ref, arrive_ref, out_ref):
    info = told_ref[runoff_ref.shape[0] :, :]
    out_ref[...] = route(runoff_ref[...] + arrive_ref[...], coefficients_of(info))


def pack_body(runoff_ref, told_ref, send_table_ref, targets_ref, arrive_ref, outgoing_ref):
    days = runoff_ref.shape[0]
    info = told_ref[days:, :]
    routed = route(runoff_ref[...] + arrive_ref[...], coefficients_of(info))
    lay_out(outgoing_ref, choose(routed, send_table_ref[...]))
    lay_out(outgoing_ref, targets_ref[...], days)


def in_thirds(values):
    high = values.astype(BF16)
    rest = values - high.astype(F32)
    middle = rest.astype(BF16)
    return [high, middle, (rest - middle.astype(F32)).astype(BF16)]


def bundle_body(told_ref, tables_ref, bundle_ref):
    rows = told_ref.shape[0]
    bundle_ref[:rows, :] = told_ref[...]
    for basin in range(tables_ref.shape[0]):
        first = rows + basin * INFO_ROWS
        bundle_ref[first : first + INFO_ROWS, :] = tables_ref[basin]


def info_table(tables):
    pieces = []
    for first in range(0, tables.shape[0], INFO_ROWS):
        info = tables[first : first + INFO_ROWS]
        reach = info[1:2].astype(jnp.int32)
        rows = [info[0:1], (reach // 16).astype(F32), (reach % 16).astype(F32)]
        for row in range(2, KNOWN):
            rows += [third.astype(F32) for third in in_thirds(info[row : row + 1])]
        rows.append(jnp.zeros((TABLE_ROWS - len(rows), reach.shape[1]), F32))
        pieces.append(jnp.concatenate(rows, axis=0).astype(BF16))
    return jnp.concatenate(pieces, axis=0)


def looked_up(table, from_basin, from_reach):
    reaches = table.shape[1]
    sublanes = lax.broadcasted_iota(jnp.int32, (reaches, reaches), 0).astype(F32)
    pick = jnp.where(sublanes == from_reach, 1.0, 0.0).astype(BF16)
    picked = jnp.dot(table, pick, preferred_element_type=F32)
    found = jnp.zeros((TABLE_ROWS, reaches), F32)
    for basin in range(table.shape[0] // TABLE_ROWS):
        here = from_basin == float(basin)
        found = found + jnp.where(here, picked[basin * TABLE_ROWS : (basin + 1) * TABLE_ROWS], 0.0)
    coefficients = tuple(
        (found[row : row + 1] + found[row + 1 : row + 2]) + found[row + 2 : row + 3]
        for row in (3, 6, 9)
    )
    return found[0:1], 16.0 * found[1:2] + found[2:3], coefficients


def by_target(values, to_basin, to_reach, basins):
    days, reaches = values.shape
    halves = in_halves(values).astype(F32)
    parts = [
        jnp.where(to_basin == float(basin), halves, 0.0).astype(BF16) for basin in range(basins)
    ]
    table = one_hot(as_column(to_reach), reaches)
    sums = jnp.dot(jnp.concatenate(parts, axis=0), table, preferred_element_type=F32)
    return [
        sums[first : first + days] + sums[first + days : first + 2 * days]
        for first in range(0, 2 * basins * days, 2 * days)
    ]


def prepare_body(between_ref, above_ref, ready_ref, paths_ref):
    basins, days, reaches = ready_ref.shape
    rows = days + INFO_ROWS
    to_basin, to_reach, coefficients = looked_up(
        info_table(between_ref[rows:, :]), above_ref[days : days + 1, :], above_ref[days + 1 : days + 2, :]
    )
    paths_ref[:rows, :] = above_ref[...]
    blank = jnp.zeros((INFO_ROWS - KNOWN, reaches), F32)
    paths_ref[rows:, :] = jnp.concatenate([to_basin, to_reach, *coefficients, blank], axis=0)
    own = between_ref[days:rows, :]
    for basin, sums in enumerate(by_target(between_ref[:days, :], own[0:1], own[1:2], basins)):
        ready_ref[basin] = sums


def pack_beyond_body(passed_ref, ready_ref, paths_ref, outgoing_ref):
    basins, days, _ = outgoing_ref.shape
    above, between = paths_ref[days : days + INFO_ROWS, :], paths_ref[days + INFO_ROWS :, :]
    outflow = paths_ref[:days, :] + route(passed_ref[...], coefficients_of(above))
    routed = route(outflow, coefficients_of(between))
    for basin, sums in enumerate(by_target(routed, between[0:1], between[1:2], basins)):
        outgoing_ref[basin] = ready_ref[basin] + sums


def add_up_body(received_ref, arrive_ref):
    total = received_ref[0]
    for basin in range(1, received_ref.shape[0]):
        total = total + received_ref[basin]
    arrive_ref[...] = total


def per_device(
    forcings, w_input, w_recur, gate_bias, w_runoff, travel_time, weight_x, drain_basin, drain_reach
):
    basins = lax.axis_size("basin")
    groups = lax.axis_size("order")
    days, channels, reaches = forcings.shape
    units = w_recur.shape[1]
    capacity = 2 * reaches // basins
    slots = basins * capacity
    split = capacity % 128 == 0

    def series():
        return jax.ShapeDtypeStruct((days, reaches), F32)

    def swap(outgoing):
        return lax.all_to_all(outgoing, "basin", split_axis=0, concat_axis=0, tiled=True)

    def exchange(outgoing):
        if split:
            return swap(outgoing)
        outgoing = outgoing.reshape(-1, basins, capacity)
        received = lax.all_to_all(outgoing, "basin", split_axis=1, concat_axis=1, tiled=True)
        return received.reshape(-1, slots)

    def row(values):
        return values.reshape(1, -1)

    operands = (
        forcings.reshape(days * channels, reaches),
        w_input.T,
        w_recur,
        row(gate_bias),
        row(w_runoff),
        row(travel_time),
        row(weight_x),
        row(drain_basin),
        row(drain_reach),
    )
    told_shape = jax.ShapeDtypeStruct((days + INFO_ROWS, reaches), F32)
    bundle_shape = jax.ShapeDtypeStruct((days + (1 + basins) * INFO_ROWS, reaches), F32)
    ready_shape = jax.ShapeDtypeStruct((basins, days, reaches), F32)
    paths_shape = jax.ShapeDtypeStruct((days + 2 * INFO_ROWS, reaches), F32)
    payload_shape = jax.ShapeDtypeStruct(
        (basins, days + ID_ROWS, capacity) if split else (days + ID_ROWS, slots), F32
    )
    runoff, told, spread, between, above, ready, paths, *late = call(
        functools.partial(first_body, days=days, basins=basins),
        [
            series(),
            told_shape,
            jax.ShapeDtypeStruct((basins, INFO_ROWS, reaches), F32),
            bundle_shape,
            told_shape,
            ready_shape,
            paths_shape,
            series(),
            series(),
            jax.ShapeDtypeStruct((reaches, slots), BF16),
            jax.ShapeDtypeStruct((ID_ROWS, slots), F32),
            payload_shape,
        ],
        megabytes=56,
        in_specs=[pl.BlockSpec(memory_space=pltpu.HBM) for _ in operands],
        scratch_shapes=[pltpu.VMEM(array.shape, array.dtype) for array in operands]
        + [
            pltpu.VMEM((units // channels, 2 * units, 4 * units), BF16),
            pltpu.VMEM((reaches, units), F32),
            pltpu.SemaphoreType.DMA((len(operands),)),
        ],
    )(*operands)

    missing, absent, send_table, targets, outgoing = late
    group = lax.axis_index("order")
    later = range(1, groups // 2)

    def moved(block, routes):
        pairs = [
            (source * basins + basin, target * basins + basin)
            for source, target in routes
            for basin in range(basins)
        ]
        return lax.ppermute(block, ("order", "basin"), pairs)

    neighbours = [(place, place ^ 1) for place in range(groups)]
    two_down = [(place, (place + 2) % groups) for place in range(groups)]

    def nothing(*_):
        return jnp.zeros((days, reaches), F32)

    above = lax.cond(
        group % 2 == 1, lambda told, blank: moved(told, two_down), lambda _, blank: blank, told, above
    )
    spread, above = lax.optimization_barrier((spread, above))
    between = lax.cond(
        (group % 2 == 0) & (group > 1),
        lambda spread, told, _: call(bundle_body, bundle_shape)(told, swap(spread)),
        lambda spread, told, blank: blank,
        spread,
        told,
        between,
    )
    outgoing, between = lax.optimization_barrier((outgoing, between))

    def deliver(outgoing, copies=1):
        return tuple(call(unpack_body, [series()] * copies)(exchange(outgoing)))

    arrive, passed = lax.cond(
        group == 0,
        lambda outgoing, *_: deliver(outgoing, 2),
        lambda outgoing, *blanks: tuple(blanks),
        outgoing,
        missing,
        absent,
    )
    arrive, passed, between = lax.optimization_barrier((arrive, passed, between))
    passed = moved(passed, [(0, 3)] if groups > 3 else [])
    between = lax.cond(
        group > 1, lambda told: moved(told, neighbours), lambda told: told, between
    )
    ready, paths = lax.cond(
        (group % 2 == 1) & (group > 1),
        lambda *known: tuple(call(prepare_body, [ready_shape, paths_shape], 24)(*known[:2])),
        lambda between, above, ready, paths: (ready, paths),
        between,
        above,
        ready,
        paths,
    )
    arrive, ready = lax.optimization_barrier((arrive, ready))
    arrive = lax.cond(
        group < 2, lambda arrive: moved(arrive, neighbours), lambda arrive: arrive, arrive
    )
    arrive = jnp.where(group == 1, arrive, 0.0)
    for pair in later:
        above, between, below = 2 * pair - 1, 2 * pair, 2 * pair + 1
        if pair > 1:
            passed = moved(arrive, two_down)
        delivered = lax.cond(
            group == above,
            lambda arrive: deliver(
                call(pack_body, payload_shape)(runoff, told, send_table, targets, arrive)
            )[0],
            nothing,
            arrive,
        )
        passed, delivered = lax.optimization_barrier((passed, delivered))
        received = lax.cond(
            group == below,
            lambda passed, _: call(add_up_body, series())(
                swap(call(pack_beyond_body, ready_shape, 24)(passed, ready, paths))
            ),
            lambda _, delivered: delivered,
            passed,
            delivered,
        )
        received = lax.cond(
            (group == above) | (group == between),
            lambda received: moved(received, [(above, between)]),
            lambda received: received,
            received,
        )
        arrive = arrive + jnp.where(group == above, 0.0, received)
    return call(route_body, series())(runoff, told, arrive)


def solution(mesh):
    return jax.shard_map(
        per_device,
        mesh=mesh,
        in_specs=(
            P(None, None, ("order", "basin")),
            P(),
            P(),
            P(),
            P(),
            P(("order", "basin")),
            P(("order", "basin")),
            P(("order", "basin"), None),
            P(("order", "basin"), None),
        ),
        out_specs=P(None, ("order", "basin")),
        check_vma=False,
    )
```

```python
import functools

import jax
import jax.numpy as jnp
from jax import lax
from jax.experimental import pallas as pl
from jax.experimental.pallas import tpu as pltpu
from jax.sharding import PartitionSpec as P

F32 = jnp.float32
BF16 = jnp.bfloat16
ID_ROWS = 8
TABLE_ROWS = 16
KNOWN = 5
INFO_ROWS = 8
CHUNK = 512


def vmem():
    return pl.BlockSpec(memory_space=pltpu.VMEM)


def call(body, out_shape, megabytes=8, **more):
    return pl.pallas_call(
        body,
        out_shape=out_shape,
        out_specs=jax.tree.map(lambda _: vmem(), out_shape),
        compiler_params=pltpu.CompilerParams(vmem_limit_bytes=megabytes << 20),
        **more,
    )


def delayed(series, days):
    return jnp.concatenate(
        [jnp.zeros((days, series.shape[1]), series.dtype), series[: series.shape[0] - days]], axis=0
    )


def routing_coefficients(travel_time, weight_x):
    held = travel_time * (1.0 - weight_x)
    denominator = held + 0.5
    coeff_first = (0.5 - travel_time * weight_x) / denominator
    coeff_second = (0.5 + travel_time * weight_x) / denominator
    recession = (held - 0.5) / denominator
    return coeff_first, coeff_first * recession + coeff_second, recession


def route(inflow, coefficients):
    first, later, recession = coefficients
    stored, power, reach = inflow, recession, 1
    while reach < inflow.shape[0]:
        stored = stored + power * delayed(stored, reach)
        power, reach = power * power, 2 * reach
    return first * inflow + later * delayed(stored, 1)


def in_halves(values):
    high = values.astype(BF16)
    return jnp.concatenate([high, (values - high.astype(F32)).astype(BF16)], axis=0)


def choose(values, table):
    both = jnp.dot(in_halves(values), table, preferred_element_type=F32)
    return both[: values.shape[0]] + both[values.shape[0] :]


def as_column(row):
    return jnp.transpose(jnp.broadcast_to(row, (8, row.shape[1])))[:, :1]


def one_hot(index_column, width):
    lanes = lax.broadcasted_iota(jnp.int32, (index_column.shape[0], width), 1).astype(F32)
    return jnp.where(index_column == lanes, 1.0, 0.0).astype(BF16)


def lay_out(ref, rows, first_row=0):
    count = rows.shape[0]
    if len(ref.shape) == 2:
        ref[first_row : first_row + count, :] = rows
    else:
        capacity = ref.shape[2]
        for basin in range(ref.shape[0]):
            ref[basin, first_row : first_row + count, :] = rows[
                :, basin * capacity : (basin + 1) * capacity
            ]


def take_in(ref, first_row, count):
    if len(ref.shape) == 2:
        return ref[first_row : first_row + count, :]
    return jnp.concatenate(
        [ref[basin, first_row : first_row + count, :] for basin in range(ref.shape[0])], axis=1
    )


def send_slots(drain_to, basins, capacity):
    reaches = drain_to.shape[1]
    basin_rows = max(basins, 8)
    member = (lax.broadcasted_iota(jnp.int32, (basin_rows, reaches), 0) == drain_to).astype(F32)
    before = lax.broadcasted_iota(jnp.int32, (reaches, reaches), 0)
    after = lax.broadcasted_iota(jnp.int32, (reaches, reaches), 1)
    upper = jnp.where(before < after, 1.0, 0.0).astype(BF16)
    earlier = jnp.dot(member.astype(BF16), upper, preferred_element_type=F32)
    rank = jnp.sum(member * earlier, axis=0, keepdims=True)
    return drain_to.astype(F32) * capacity + rank


def slot_tables(drain_to, reach, basins, capacity):
    send_table = one_hot(as_column(send_slots(drain_to, basins, capacity)), basins * capacity)
    digits = jnp.concatenate(
        [reach // 16, reach % 16, jnp.zeros((6, reach.shape[1]), jnp.int32)], axis=0
    )
    found = jnp.dot(digits.astype(F32).astype(BF16), send_table, preferred_element_type=F32)
    return send_table, jnp.broadcast_to(
        16.0 * found[0:1] + found[1:2], (ID_ROWS, send_table.shape[1])
    )


def known(drain_basin, drain_reach, travel_time, weight_x):
    rows = (drain_basin.astype(F32), drain_reach.astype(F32))
    rows += routing_coefficients(travel_time, weight_x)
    blank = jnp.zeros((INFO_ROWS - len(rows), travel_time.shape[1]), F32)
    return jnp.concatenate([*rows, blank], axis=0)


def coefficients_of(info):
    return tuple(info[row : row + 1, :] for row in range(2, KNOWN))


def first_body(
    forcings_hbm,
    w_input_hbm,
    w_recur_hbm,
    gate_bias_hbm,
    w_runoff_hbm,
    travel_hbm,
    weight_hbm,
    drain_basin_hbm,
    drain_reach_hbm,
    runoff_ref,
    told_ref,
    spread_ref,
    between_ref,
    above_ref,
    ready_ref,
    paths_ref,
    missing_ref,
    absent_ref,
    send_table_ref,
    targets_ref,
    outgoing_ref,
    forcings_ref,
    w_input_ref,
    w_recur_ref,
    gate_bias_ref,
    w_runoff_ref,
    travel_ref,
    weight_ref,
    drain_basin_ref,
    drain_reach_ref,
    weights,
    sums,
    arrived,
    *,
    days,
    basins,
):
    loads = [
        pltpu.make_async_copy(source, target, arrived.at[number])
        for number, (source, target) in enumerate(
            [
                (w_recur_hbm, w_recur_ref),
                (w_input_hbm, w_input_ref),
                (gate_bias_hbm, gate_bias_ref),
                (w_runoff_hbm, w_runoff_ref),
                (travel_hbm, travel_ref),
                (weight_hbm, weight_ref),
                (drain_basin_hbm, drain_basin_ref),
                (drain_reach_hbm, drain_reach_ref),
                (forcings_hbm, forcings_ref),
            ]
        )
    ]
    for load in loads:
        load.start()
    reaches = forcings_ref.shape[1]
    channels = forcings_ref.shape[0] // days
    units = w_recur_ref.shape[1]
    gates = 4 * units
    per_block = units // channels
    capacity = 2 * reaches // basins
    for day in range(per_block):
        weights[day, units:, :] = jnp.zeros((units, gates), BF16)
    for load in loads[:-1]:
        load.wait()

    gate_lane = lax.broadcasted_iota(jnp.int32, (1, gates), 1)
    is_candidate = (gate_lane >= 2 * units) & (gate_lane < 3 * units)
    scale = jnp.where(is_candidate, 1.0, 0.5)
    recur = (jnp.transpose(w_recur_ref[...].astype(F32)) * (0.5 * scale)).astype(BF16)
    inputs = (w_input_ref[...].astype(F32) * scale).astype(BF16)
    bias = gate_bias_ref[...] * scale
    readout = as_column(0.5 * w_runoff_ref[...])
    for day in range(per_block):
        weights[day, :units, :] = recur
        weights[day, units + day * channels : units + (day + 1) * channels, :] = inputs
    chunk = min(CHUNK, reaches)
    chunks = reaches // chunk

    info = known(drain_basin_ref[...], drain_reach_ref[...], travel_ref[...], weight_ref[...])
    told_ref[days:, :] = info
    for basin in range(basins):
        spread_ref[basin] = info
    send_table, targets = slot_tables(drain_basin_ref[...], drain_reach_ref[...], basins, capacity)
    send_table_ref[...] = send_table
    targets_ref[...] = targets
    for blank_ref in (between_ref, above_ref, ready_ref, paths_ref, missing_ref, absent_ref):
        blank_ref[...] = jnp.zeros_like(blank_ref)
    loads[-1].wait()

    state = [
        (jnp.zeros((chunk, units), BF16), jnp.zeros((chunk, units), F32)) for _ in range(chunks)
    ]
    for block in range(days // per_block):
        rows = slice(block * units, (block + 1) * units)
        forced = jnp.transpose(forcings_ref[rows, :].astype(F32)).astype(BF16)
        for day in range(per_block):
            for part in range(chunks):
                hidden, memory = state[part]
                span = slice(part * chunk, (part + 1) * chunk)
                gate_sums = bias + jnp.dot(
                    jnp.concatenate([hidden, forced[span]], axis=1),
                    weights[day],
                    preferred_element_type=F32,
                )
                ingate = jnp.tanh(gate_sums[:, :units])
                forget = jnp.tanh(gate_sums[:, units : 2 * units])
                candidate = jnp.tanh(gate_sums[:, 2 * units : 3 * units])
                outgate = jnp.tanh(gate_sums[:, 3 * units :])
                memory = 0.5 * ((forget * memory + memory) + (ingate * candidate + candidate))
                squashed = jnp.tanh(memory)
                hidden = (outgate * squashed + squashed).astype(BF16)
                drained = jnp.sum(
                    jnp.transpose(hidden).astype(F32) * readout, axis=0, keepdims=True
                )
                now = block * per_block + day
                sums[now : now + 1, span] = drained
                state[part] = (hidden, memory)
    pre = sums[...]
    runoff = jnp.maximum(pre, 0.0) + jnp.log1p(jnp.exp(-jnp.abs(pre)))
    runoff_ref[...] = runoff
    routed = route(runoff, coefficients_of(info))
    told_ref[:days, :] = routed
    lay_out(outgoing_ref, choose(routed, send_table_ref[...]))
    lay_out(outgoing_ref, targets_ref[...], days)


def unpack_body(received_ref, *arrive_refs):
    days, reaches = arrive_refs[0].shape
    recv_table = one_hot(as_column(take_in(received_ref, days, 1)), reaches)
    arrive = choose(take_in(received_ref, 0, days), recv_table)
    for arrive_ref in arrive_refs:
        arrive_ref[...] = arrive


def route_body(runoff_ref, told_ref, arrive_ref, out_ref):
    info = told_ref[runoff_ref.shape[0] :, :]
    out_ref[...] = route(runoff_ref[...] + arrive_ref[...], coefficients_of(info))


def pack_body(runoff_ref, told_ref, send_table_ref, targets_ref, arrive_ref, outgoing_ref):
    days = runoff_ref.shape[0]
    info = told_ref[days:, :]
    routed = route(runoff_ref[...] + arrive_ref[...], coefficients_of(info))
    lay_out(outgoing_ref, choose(routed, send_table_ref[...]))
    lay_out(outgoing_ref, targets_ref[...], days)


def in_thirds(values):
    high = values.astype(BF16)
    rest = values - high.astype(F32)
    middle = rest.astype(BF16)
    return [high, middle, (rest - middle.astype(F32)).astype(BF16)]


def bundle_body(told_ref, tables_ref, bundle_ref):
    rows = told_ref.shape[0]
    bundle_ref[:rows, :] = told_ref[...]
    for basin in range(tables_ref.shape[0]):
        first = rows + basin * INFO_ROWS
        bundle_ref[first : first + INFO_ROWS, :] = tables_ref[basin]


def info_table(tables):
    pieces = []
    for first in range(0, tables.shape[0], INFO_ROWS):
        info = tables[first : first + INFO_ROWS]
        reach = info[1:2].astype(jnp.int32)
        rows = [info[0:1], (reach // 16).astype(F32), (reach % 16).astype(F32)]
        for row in range(2, KNOWN):
            rows += [third.astype(F32) for third in in_thirds(info[row : row + 1])]
        rows.append(jnp.zeros((TABLE_ROWS - len(rows), reach.shape[1]), F32))
        pieces.append(jnp.concatenate(rows, axis=0).astype(BF16))
    return jnp.concatenate(pieces, axis=0)


def looked_up(table, from_basin, from_reach):
    reaches = table.shape[1]
    sublanes = lax.broadcasted_iota(jnp.int32, (reaches, reaches), 0).astype(F32)
    pick = jnp.where(sublanes == from_reach, 1.0, 0.0).astype(BF16)
    picked = jnp.dot(table, pick, preferred_element_type=F32)
    found = jnp.zeros((TABLE_ROWS, reaches), F32)
    for basin in range(table.shape[0] // TABLE_ROWS):
        here = from_basin == float(basin)
        found = found + jnp.where(here, picked[basin * TABLE_ROWS : (basin + 1) * TABLE_ROWS], 0.0)
    coefficients = tuple(
        (found[row : row + 1] + found[row + 1 : row + 2]) + found[row + 2 : row + 3]
        for row in (3, 6, 9)
    )
    return found[0:1], 16.0 * found[1:2] + found[2:3], coefficients


def by_target(values, to_basin, to_reach, basins):
    days, reaches = values.shape
    halves = in_halves(values).astype(F32)
    parts = [
        jnp.where(to_basin == float(basin), halves, 0.0).astype(BF16) for basin in range(basins)
    ]
    table = one_hot(as_column(to_reach), reaches)
    sums = jnp.dot(jnp.concatenate(parts, axis=0), table, preferred_element_type=F32)
    return [
        sums[first : first + days] + sums[first + days : first + 2 * days]
        for first in range(0, 2 * basins * days, 2 * days)
    ]


def prepare_body(between_ref, above_ref, ready_ref, paths_ref):
    basins, days, reaches = ready_ref.shape
    rows = days + INFO_ROWS
    to_basin, to_reach, coefficients = looked_up(
        info_table(between_ref[rows:, :]), above_ref[days : days + 1, :], above_ref[days + 1 : days + 2, :]
    )
    paths_ref[:rows, :] = above_ref[...]
    blank = jnp.zeros((INFO_ROWS - KNOWN, reaches), F32)
    paths_ref[rows:, :] = jnp.concatenate([to_basin, to_reach, *coefficients, blank], axis=0)
    own = between_ref[days:rows, :]
    for basin, sums in enumerate(by_target(between_ref[:days, :], own[0:1], own[1:2], basins)):
        ready_ref[basin] = sums


def pack_beyond_body(passed_ref, ready_ref, paths_ref, outgoing_ref):
    basins, days, _ = outgoing_ref.shape
    above, between = paths_ref[days : days + INFO_ROWS, :], paths_ref[days + INFO_ROWS :, :]
    outflow = paths_ref[:days, :] + route(passed_ref[...], coefficients_of(above))
    routed = route(outflow, coefficients_of(between))
    for basin, sums in enumerate(by_target(routed, between[0:1], between[1:2], basins)):
        outgoing_ref[basin] = ready_ref[basin] + sums


def add_up_body(received_ref, arrive_ref):
    total = received_ref[0]
    for basin in range(1, received_ref.shape[0]):
        total = total + received_ref[basin]
    arrive_ref[...] = total


def per_device(
    forcings, w_input, w_recur, gate_bias, w_runoff, travel_time, weight_x, drain_basin, drain_reach
):
    basins = lax.axis_size("basin")
    groups = lax.axis_size("order")
    days, channels, reaches = forcings.shape
    units = w_recur.shape[1]
    capacity = 2 * reaches // basins
    slots = basins * capacity
    split = capacity % 128 == 0

    def series():
        return jax.ShapeDtypeStruct((days, reaches), F32)

    def swap(outgoing):
        return lax.all_to_all(outgoing, "basin", split_axis=0, concat_axis=0, tiled=True)

    def exchange(outgoing):
        if split:
            return swap(outgoing)
        outgoing = outgoing.reshape(-1, basins, capacity)
        received = lax.all_to_all(outgoing, "basin", split_axis=1, concat_axis=1, tiled=True)
        return received.reshape(-1, slots)

    def row(values):
        return values.reshape(1, -1)

    operands = (
        forcings.reshape(days * channels, reaches),
        w_input.T,
        w_recur,
        row(gate_bias),
        row(w_runoff),
        row(travel_time),
        row(weight_x),
        row(drain_basin),
        row(drain_reach),
    )
    told_shape = jax.ShapeDtypeStruct((days + INFO_ROWS, reaches), F32)
    bundle_shape = jax.ShapeDtypeStruct((days + (1 + basins) * INFO_ROWS, reaches), F32)
    ready_shape = jax.ShapeDtypeStruct((basins, days, reaches), F32)
    paths_shape = jax.ShapeDtypeStruct((days + 2 * INFO_ROWS, reaches), F32)
    payload_shape = jax.ShapeDtypeStruct(
        (basins, days + ID_ROWS, capacity) if split else (days + ID_ROWS, slots), F32
    )
    runoff, told, spread, between, above, ready, paths, *late = call(
        functools.partial(first_body, days=days, basins=basins),
        [
            series(),
            told_shape,
            jax.ShapeDtypeStruct((basins, INFO_ROWS, reaches), F32),
            bundle_shape,
            told_shape,
            ready_shape,
            paths_shape,
            series(),
            series(),
            jax.ShapeDtypeStruct((reaches, slots), BF16),
            jax.ShapeDtypeStruct((ID_ROWS, slots), F32),
            payload_shape,
        ],
        megabytes=56,
        in_specs=[pl.BlockSpec(memory_space=pltpu.HBM) for _ in operands],
        scratch_shapes=[pltpu.VMEM(array.shape, array.dtype) for array in operands]
        + [
            pltpu.VMEM((units // channels, 2 * units, 4 * units), BF16),
            pltpu.VMEM((days, reaches), F32),
            pltpu.SemaphoreType.DMA((len(operands),)),
        ],
    )(*operands)

    missing, absent, send_table, targets, outgoing = late
    group = lax.axis_index("order")
    later = range(1, groups // 2)

    def moved(block, routes):
        pairs = [
            (source * basins + basin, target * basins + basin)
            for source, target in routes
            for basin in range(basins)
        ]
        return lax.ppermute(block, ("order", "basin"), pairs)

    neighbours = [(place, place ^ 1) for place in range(groups)]
    two_down = [(place, (place + 2) % groups) for place in range(groups)]

    def nothing(*_):
        return jnp.zeros((days, reaches), F32)

    above = lax.cond(
        group % 2 == 1, lambda told, blank: moved(told, two_down), lambda _, blank: blank, told, above
    )
    spread, above = lax.optimization_barrier((spread, above))
    between = lax.cond(
        (group % 2 == 0) & (group > 1),
        lambda spread, told, _: call(bundle_body, bundle_shape)(told, swap(spread)),
        lambda spread, told, blank: blank,
        spread,
        told,
        between,
    )
    outgoing, between = lax.optimization_barrier((outgoing, between))

    def deliver(outgoing, copies=1):
        return tuple(call(unpack_body, [series()] * copies)(exchange(outgoing)))

    arrive, passed = lax.cond(
        group == 0,
        lambda outgoing, *_: deliver(outgoing, 2),
        lambda outgoing, *blanks: tuple(blanks),
        outgoing,
        missing,
        absent,
    )
    arrive, passed, between = lax.optimization_barrier((arrive, passed, between))
    passed = moved(passed, [(place, place ^ 3) for place in range(groups)])
    between = lax.cond(
        group > 1, lambda told: moved(told, neighbours), lambda told: told, between
    )
    ready, paths = lax.cond(
        (group % 2 == 1) & (group > 1),
        lambda *known: tuple(call(prepare_body, [ready_shape, paths_shape], 24)(*known[:2])),
        lambda between, above, ready, paths: (ready, paths),
        between,
        above,
        ready,
        paths,
    )
    arrive, ready = lax.optimization_barrier((arrive, ready))
    arrive = lax.cond(
        group < 2, lambda arrive: moved(arrive, neighbours), lambda arrive: arrive, arrive
    )
    arrive = jnp.where(group == 1, arrive, 0.0)
    for pair in later:
        above, between, below = 2 * pair - 1, 2 * pair, 2 * pair + 1
        if pair > 1:
            passed = moved(arrive, two_down)
        delivered = lax.cond(
            group == above,
            lambda arrive: deliver(
                call(pack_body, payload_shape)(runoff, told, send_table, targets, arrive)
            )[0],
            nothing,
            arrive,
        )
        passed, delivered = lax.optimization_barrier((passed, delivered))
        received = lax.cond(
            group == below,
            lambda passed, _: call(add_up_body, series())(
                swap(call(pack_beyond_body, ready_shape, 24)(passed, ready, paths))
            ),
            lambda _, delivered: delivered,
            passed,
            delivered,
        )
        received = lax.cond(
            (group == above) | (group == between),
            lambda received: moved(received, [(above, between)]),
            lambda received: received,
            received,
        )
        arrive = arrive + jnp.where(group == above, 0.0, received)
    return call(route_body, series())(runoff, told, arrive)


def solution(mesh):
    return jax.shard_map(
        per_device,
        mesh=mesh,
        in_specs=(
            P(None, None, ("order", "basin")),
            P(),
            P(),
            P(),
            P(),
            P(("order", "basin")),
            P(("order", "basin")),
            P(("order", "basin"), None),
            P(("order", "basin"), None),
        ),
        out_specs=P(None, ("order", "basin")),
        check_vma=False,
    )
```

```python
import functools

import jax
import jax.numpy as jnp
from jax import lax
from jax.experimental import pallas as pl
from jax.experimental.pallas import tpu as pltpu
from jax.sharding import PartitionSpec as P

F32 = jnp.float32
BF16 = jnp.bfloat16
ID_ROWS = 8
TABLE_ROWS = 16
KNOWN = 5
INFO_ROWS = 8
CHUNK = 512


def vmem():
    return pl.BlockSpec(memory_space=pltpu.VMEM)


def call(body, out_shape, megabytes=8, **more):
    return pl.pallas_call(
        body,
        out_shape=out_shape,
        out_specs=jax.tree.map(lambda _: vmem(), out_shape),
        compiler_params=pltpu.CompilerParams(vmem_limit_bytes=megabytes << 20),
        **more,
    )


def delayed(series, days):
    return jnp.concatenate(
        [jnp.zeros((days, series.shape[1]), series.dtype), series[: series.shape[0] - days]], axis=0
    )


def routing_coefficients(travel_time, weight_x):
    held = travel_time * (1.0 - weight_x)
    denominator = held + 0.5
    coeff_first = (0.5 - travel_time * weight_x) / denominator
    coeff_second = (0.5 + travel_time * weight_x) / denominator
    recession = (held - 0.5) / denominator
    return coeff_first, coeff_first * recession + coeff_second, recession


def route(inflow, coefficients):
    first, later, recession = coefficients
    stored, power, reach = inflow, recession, 1
    while reach < inflow.shape[0]:
        stored = stored + power * delayed(stored, reach)
        power, reach = power * power, 2 * reach
    return first * inflow + later * delayed(stored, 1)


def in_halves(values):
    high = values.astype(BF16)
    return jnp.concatenate([high, (values - high.astype(F32)).astype(BF16)], axis=0)


def choose(values, table):
    both = jnp.dot(in_halves(values), table, preferred_element_type=F32)
    return both[: values.shape[0]] + both[values.shape[0] :]


def as_column(row):
    return jnp.transpose(jnp.broadcast_to(row, (8, row.shape[1])))[:, :1]


def one_hot(index_column, width):
    lanes = lax.broadcasted_iota(jnp.int32, (index_column.shape[0], width), 1).astype(F32)
    return jnp.where(index_column == lanes, 1.0, 0.0).astype(BF16)


def lay_out(ref, rows, first_row=0):
    count = rows.shape[0]
    if len(ref.shape) == 2:
        ref[first_row : first_row + count, :] = rows
    else:
        capacity = ref.shape[2]
        for basin in range(ref.shape[0]):
            ref[basin, first_row : first_row + count, :] = rows[
                :, basin * capacity : (basin + 1) * capacity
            ]


def take_in(ref, first_row, count):
    if len(ref.shape) == 2:
        return ref[first_row : first_row + count, :]
    return jnp.concatenate(
        [ref[basin, first_row : first_row + count, :] for basin in range(ref.shape[0])], axis=1
    )


def send_slots(drain_to, basins, capacity):
    reaches = drain_to.shape[1]
    basin_rows = max(basins, 8)
    member = (lax.broadcasted_iota(jnp.int32, (basin_rows, reaches), 0) == drain_to).astype(F32)
    before = lax.broadcasted_iota(jnp.int32, (reaches, reaches), 0)
    after = lax.broadcasted_iota(jnp.int32, (reaches, reaches), 1)
    upper = jnp.where(before < after, 1.0, 0.0).astype(BF16)
    earlier = jnp.dot(member.astype(BF16), upper, preferred_element_type=F32)
    rank = jnp.sum(member * earlier, axis=0, keepdims=True)
    return drain_to.astype(F32) * capacity + rank


def slot_tables(drain_to, reach, basins, capacity):
    send_table = one_hot(as_column(send_slots(drain_to, basins, capacity)), basins * capacity)
    digits = jnp.concatenate(
        [reach // 16, reach % 16, jnp.zeros((6, reach.shape[1]), jnp.int32)], axis=0
    )
    found = jnp.dot(digits.astype(F32).astype(BF16), send_table, preferred_element_type=F32)
    return send_table, jnp.broadcast_to(
        16.0 * found[0:1] + found[1:2], (ID_ROWS, send_table.shape[1])
    )


def known(drain_basin, drain_reach, travel_time, weight_x):
    rows = (drain_basin.astype(F32), drain_reach.astype(F32))
    rows += routing_coefficients(travel_time, weight_x)
    blank = jnp.zeros((INFO_ROWS - len(rows), travel_time.shape[1]), F32)
    return jnp.concatenate([*rows, blank], axis=0)


def coefficients_of(info):
    return tuple(info[row : row + 1, :] for row in range(2, KNOWN))


def first_body(
    forcings_hbm,
    w_input_hbm,
    w_recur_hbm,
    gate_bias_hbm,
    w_runoff_hbm,
    travel_hbm,
    weight_hbm,
    drain_basin_hbm,
    drain_reach_hbm,
    runoff_ref,
    told_ref,
    spread_ref,
    between_ref,
    above_ref,
    ready_ref,
    paths_ref,
    missing_ref,
    absent_ref,
    send_table_ref,
    targets_ref,
    outgoing_ref,
    forcings_ref,
    w_input_ref,
    w_recur_ref,
    gate_bias_ref,
    w_runoff_ref,
    travel_ref,
    weight_ref,
    drain_basin_ref,
    drain_reach_ref,
    weights,
    sums,
    arrived,
    *,
    days,
    basins,
):
    loads = [
        pltpu.make_async_copy(source, target, arrived.at[number])
        for number, (source, target) in enumerate(
            [
                (w_recur_hbm, w_recur_ref),
                (w_input_hbm, w_input_ref),
                (gate_bias_hbm, gate_bias_ref),
                (w_runoff_hbm, w_runoff_ref),
                (travel_hbm, travel_ref),
                (weight_hbm, weight_ref),
                (drain_basin_hbm, drain_basin_ref),
                (drain_reach_hbm, drain_reach_ref),
                (forcings_hbm, forcings_ref),
            ]
        )
    ]
    for load in loads:
        load.start()
    reaches = forcings_ref.shape[1]
    channels = forcings_ref.shape[0] // days
    units = w_recur_ref.shape[1]
    gates = 4 * units
    per_block = units // channels - 1
    capacity = 2 * reaches // basins
    for day in range(per_block):
        weights[day, units:, :] = jnp.zeros((units, gates), BF16)
    for blank_ref in (between_ref, above_ref, ready_ref, paths_ref, missing_ref, absent_ref):
        blank_ref[...] = jnp.zeros_like(blank_ref)
    for load in loads[:-1]:
        load.wait()

    gate_lane = lax.broadcasted_iota(jnp.int32, (1, gates), 1)
    is_candidate = (gate_lane >= 2 * units) & (gate_lane < 3 * units)
    scale = jnp.where(is_candidate, 1.0, 0.5)
    recur = (jnp.transpose(w_recur_ref[...].astype(F32)) * (0.5 * scale)).astype(BF16)
    inputs = (w_input_ref[...].astype(F32) * scale).astype(BF16)
    thirds = [third.astype(F32) for third in in_thirds(gate_bias_ref[...] * scale)]
    blank = jnp.zeros((channels - len(thirds), gates), F32)
    biases = jnp.concatenate([*thirds, blank], axis=0).astype(BF16)
    readout = as_column(0.5 * w_runoff_ref[...])
    for day in range(per_block):
        weights[day, :units, :] = recur
        weights[day, units + day * channels : units + (day + 1) * channels, :] = inputs
        weights[day, units + per_block * channels :, :] = biases
    chunk = min(CHUNK, reaches)
    chunks = reaches // chunk

    info = known(drain_basin_ref[...], drain_reach_ref[...], travel_ref[...], weight_ref[...])
    told_ref[days:, :] = info
    for basin in range(basins):
        spread_ref[basin] = info
    send_table, targets = slot_tables(drain_basin_ref[...], drain_reach_ref[...], basins, capacity)
    send_table_ref[...] = send_table
    targets_ref[...] = targets
    loads[-1].wait()

    state = [
        (jnp.zeros((chunk, units), BF16), jnp.zeros((chunk, units), F32)) for _ in range(chunks)
    ]
    for first in range(0, days, per_block):
        count = min(per_block, days - first)
        forced = [forcings_ref[first * channels : (first + count) * channels, :].astype(F32)]
        if count < per_block:
            forced.append(jnp.zeros(((per_block - count) * channels, reaches), F32))
        forced.append(jnp.ones((channels, reaches), F32))
        forced = jnp.transpose(jnp.concatenate(forced, axis=0)).astype(BF16)
        for day in range(count):
            for part in range(chunks):
                hidden, memory = state[part]
                span = slice(part * chunk, (part + 1) * chunk)
                gate_sums = jnp.dot(
                    jnp.concatenate([hidden, forced[span]], axis=1),
                    weights[day],
                    preferred_element_type=F32,
                )
                ingate = jnp.tanh(gate_sums[:, :units])
                forget = jnp.tanh(gate_sums[:, units : 2 * units])
                candidate = jnp.tanh(gate_sums[:, 2 * units : 3 * units])
                outgate = jnp.tanh(gate_sums[:, 3 * units :])
                memory = 0.5 * ((forget * memory + memory) + (ingate * candidate + candidate))
                squashed = jnp.tanh(memory)
                hidden = (outgate * squashed + squashed).astype(BF16)
                drained = jnp.sum(
                    jnp.transpose(hidden).astype(F32) * readout, axis=0, keepdims=True
                )
                sums[first + day : first + day + 1, span] = drained
                state[part] = (hidden, memory)
    pre = sums[...]
    runoff = jnp.maximum(pre, 0.0) + jnp.log1p(jnp.exp(-jnp.abs(pre)))
    runoff_ref[...] = runoff
    routed = route(runoff, coefficients_of(info))
    told_ref[:days, :] = routed
    lay_out(outgoing_ref, choose(routed, send_table_ref[...]))
    lay_out(outgoing_ref, targets_ref[...], days)


def unpack_body(received_ref, *arrive_refs):
    days, reaches = arrive_refs[0].shape
    recv_table = one_hot(as_column(take_in(received_ref, days, 1)), reaches)
    arrive = choose(take_in(received_ref, 0, days), recv_table)
    for arrive_ref in arrive_refs:
        arrive_ref[...] = arrive


def route_body(runoff_ref, told_ref, arrive_ref, out_ref):
    info = told_ref[runoff_ref.shape[0] :, :]
    out_ref[...] = route(runoff_ref[...] + arrive_ref[...], coefficients_of(info))


def pack_body(runoff_ref, told_ref, send_table_ref, targets_ref, arrive_ref, outgoing_ref):
    days = runoff_ref.shape[0]
    info = told_ref[days:, :]
    routed = route(runoff_ref[...] + arrive_ref[...], coefficients_of(info))
    lay_out(outgoing_ref, choose(routed, send_table_ref[...]))
    lay_out(outgoing_ref, targets_ref[...], days)


def in_thirds(values):
    high = values.astype(BF16)
    rest = values - high.astype(F32)
    middle = rest.astype(BF16)
    return [high, middle, (rest - middle.astype(F32)).astype(BF16)]


def bundle_body(told_ref, tables_ref, bundle_ref):
    rows = told_ref.shape[0]
    bundle_ref[:rows, :] = told_ref[...]
    for basin in range(tables_ref.shape[0]):
        first = rows + basin * INFO_ROWS
        bundle_ref[first : first + INFO_ROWS, :] = tables_ref[basin]


def info_table(tables):
    pieces = []
    for first in range(0, tables.shape[0], INFO_ROWS):
        info = tables[first : first + INFO_ROWS]
        reach = info[1:2].astype(jnp.int32)
        rows = [info[0:1], (reach // 16).astype(F32), (reach % 16).astype(F32)]
        for row in range(2, KNOWN):
            rows += [third.astype(F32) for third in in_thirds(info[row : row + 1])]
        rows.append(jnp.zeros((TABLE_ROWS - len(rows), reach.shape[1]), F32))
        pieces.append(jnp.concatenate(rows, axis=0).astype(BF16))
    return jnp.concatenate(pieces, axis=0)


def looked_up(table, from_basin, from_reach):
    reaches = table.shape[1]
    sublanes = lax.broadcasted_iota(jnp.int32, (reaches, reaches), 0).astype(F32)
    pick = jnp.where(sublanes == from_reach, 1.0, 0.0).astype(BF16)
    picked = jnp.dot(table, pick, preferred_element_type=F32)
    found = jnp.zeros((TABLE_ROWS, reaches), F32)
    for basin in range(table.shape[0] // TABLE_ROWS):
        here = from_basin == float(basin)
        found = found + jnp.where(here, picked[basin * TABLE_ROWS : (basin + 1) * TABLE_ROWS], 0.0)
    coefficients = tuple(
        (found[row : row + 1] + found[row + 1 : row + 2]) + found[row + 2 : row + 3]
        for row in (3, 6, 9)
    )
    return found[0:1], 16.0 * found[1:2] + found[2:3], coefficients


def by_target(values, to_basin, to_reach, basins):
    days, reaches = values.shape
    halves = in_halves(values).astype(F32)
    parts = [
        jnp.where(to_basin == float(basin), halves, 0.0).astype(BF16) for basin in range(basins)
    ]
    table = one_hot(as_column(to_reach), reaches)
    sums = jnp.dot(jnp.concatenate(parts, axis=0), table, preferred_element_type=F32)
    return [
        sums[first : first + days] + sums[first + days : first + 2 * days]
        for first in range(0, 2 * basins * days, 2 * days)
    ]


def prepare_body(between_ref, above_ref, ready_ref, paths_ref):
    basins, days, reaches = ready_ref.shape
    rows = days + INFO_ROWS
    to_basin, to_reach, coefficients = looked_up(
        info_table(between_ref[rows:, :]), above_ref[days : days + 1, :], above_ref[days + 1 : days + 2, :]
    )
    paths_ref[:rows, :] = above_ref[...]
    blank = jnp.zeros((INFO_ROWS - KNOWN, reaches), F32)
    paths_ref[rows:, :] = jnp.concatenate([to_basin, to_reach, *coefficients, blank], axis=0)
    own = between_ref[days:rows, :]
    for basin, sums in enumerate(by_target(between_ref[:days, :], own[0:1], own[1:2], basins)):
        ready_ref[basin] = sums


def pack_beyond_body(passed_ref, ready_ref, paths_ref, outgoing_ref):
    basins, days, _ = outgoing_ref.shape
    above, between = paths_ref[days : days + INFO_ROWS, :], paths_ref[days + INFO_ROWS :, :]
    outflow = paths_ref[:days, :] + route(passed_ref[...], coefficients_of(above))
    routed = route(outflow, coefficients_of(between))
    for basin, sums in enumerate(by_target(routed, between[0:1], between[1:2], basins)):
        outgoing_ref[basin] = ready_ref[basin] + sums


def add_up_body(received_ref, arrive_ref):
    total = received_ref[0]
    for basin in range(1, received_ref.shape[0]):
        total = total + received_ref[basin]
    arrive_ref[...] = total


def per_device(
    forcings, w_input, w_recur, gate_bias, w_runoff, travel_time, weight_x, drain_basin, drain_reach
):
    basins = lax.axis_size("basin")
    groups = lax.axis_size("order")
    days, channels, reaches = forcings.shape
    units = w_recur.shape[1]
    capacity = 2 * reaches // basins
    slots = basins * capacity
    split = capacity % 128 == 0

    def series():
        return jax.ShapeDtypeStruct((days, reaches), F32)

    def swap(outgoing):
        return lax.all_to_all(outgoing, "basin", split_axis=0, concat_axis=0, tiled=True)

    def exchange(outgoing):
        if split:
            return swap(outgoing)
        outgoing = outgoing.reshape(-1, basins, capacity)
        received = lax.all_to_all(outgoing, "basin", split_axis=1, concat_axis=1, tiled=True)
        return received.reshape(-1, slots)

    def row(values):
        return values.reshape(1, -1)

    operands = (
        forcings.reshape(days * channels, reaches),
        w_input.T,
        w_recur,
        row(gate_bias),
        row(w_runoff),
        row(travel_time),
        row(weight_x),
        row(drain_basin),
        row(drain_reach),
    )
    told_shape = jax.ShapeDtypeStruct((days + INFO_ROWS, reaches), F32)
    bundle_shape = jax.ShapeDtypeStruct((days + (1 + basins) * INFO_ROWS, reaches), F32)
    ready_shape = jax.ShapeDtypeStruct((basins, days, reaches), F32)
    paths_shape = jax.ShapeDtypeStruct((days + 2 * INFO_ROWS, reaches), F32)
    payload_shape = jax.ShapeDtypeStruct(
        (basins, days + ID_ROWS, capacity) if split else (days + ID_ROWS, slots), F32
    )
    runoff, told, spread, between, above, ready, paths, *late = call(
        functools.partial(first_body, days=days, basins=basins),
        [
            series(),
            told_shape,
            jax.ShapeDtypeStruct((basins, INFO_ROWS, reaches), F32),
            bundle_shape,
            told_shape,
            ready_shape,
            paths_shape,
            series(),
            series(),
            jax.ShapeDtypeStruct((reaches, slots), BF16),
            jax.ShapeDtypeStruct((ID_ROWS, slots), F32),
            payload_shape,
        ],
        megabytes=56,
        in_specs=[pl.BlockSpec(memory_space=pltpu.HBM) for _ in operands],
        scratch_shapes=[pltpu.VMEM(array.shape, array.dtype) for array in operands]
        + [
            pltpu.VMEM((units // channels - 1, 2 * units, 4 * units), BF16),
            pltpu.VMEM((days, reaches), F32),
            pltpu.SemaphoreType.DMA((len(operands),)),
        ],
    )(*operands)

    missing, absent, send_table, targets, outgoing = late
    group = lax.axis_index("order")
    later = range(1, groups // 2)

    def moved(block, routes):
        pairs = [
            (source * basins + basin, target * basins + basin)
            for source, target in routes
            for basin in range(basins)
        ]
        return lax.ppermute(block, ("order", "basin"), pairs)

    neighbours = [(place, place ^ 1) for place in range(groups)]
    two_down = [(place, (place + 2) % groups) for place in range(groups)]

    def nothing(*_):
        return jnp.zeros((days, reaches), F32)

    above = lax.cond(
        group % 2 == 1, lambda told, blank: moved(told, two_down), lambda _, blank: blank, told, above
    )
    spread, above = lax.optimization_barrier((spread, above))
    between = lax.cond(
        (group % 2 == 0) & (group > 1),
        lambda spread, told, _: call(bundle_body, bundle_shape)(told, swap(spread)),
        lambda spread, told, blank: blank,
        spread,
        told,
        between,
    )
    outgoing, between = lax.optimization_barrier((outgoing, between))

    def deliver(outgoing, copies=1):
        return tuple(call(unpack_body, [series()] * copies)(exchange(outgoing)))

    arrive, passed = lax.cond(
        group == 0,
        lambda outgoing, *_: deliver(outgoing, 2),
        lambda outgoing, *blanks: tuple(blanks),
        outgoing,
        missing,
        absent,
    )
    arrive, passed, between = lax.optimization_barrier((arrive, passed, between))
    passed = moved(passed, [(place, place ^ 3) for place in range(groups)])
    between = lax.cond(
        group > 1, lambda told: moved(told, neighbours), lambda told: told, between
    )
    ready, paths = lax.cond(
        (group % 2 == 1) & (group > 1),
        lambda *known: tuple(call(prepare_body, [ready_shape, paths_shape], 24)(*known[:2])),
        lambda between, above, ready, paths: (ready, paths),
        between,
        above,
        ready,
        paths,
    )
    arrive, ready = lax.optimization_barrier((arrive, ready))
    arrive = lax.cond(
        group < 2, lambda arrive: moved(arrive, neighbours), lambda arrive: arrive, arrive
    )
    arrive = jnp.where(group == 1, arrive, 0.0)
    for pair in later:
        above, between, below = 2 * pair - 1, 2 * pair, 2 * pair + 1
        if pair > 1:
            passed = moved(arrive, two_down)
        delivered = lax.cond(
            group == above,
            lambda arrive: deliver(
                call(pack_body, payload_shape)(runoff, told, send_table, targets, arrive)
            )[0],
            nothing,
            arrive,
        )
        passed, delivered = lax.optimization_barrier((passed, delivered))
        received = lax.cond(
            group == below,
            lambda passed, _: call(add_up_body, series())(
                swap(call(pack_beyond_body, ready_shape, 24)(passed, ready, paths))
            ),
            lambda _, delivered: delivered,
            passed,
            delivered,
        )
        received = lax.cond(
            (group == above) | (group == between),
            lambda received: moved(received, [(above, between)]),
            lambda received: received,
            received,
        )
        arrive = arrive + jnp.where(group == above, 0.0, received)
    return call(route_body, series())(runoff, told, arrive)


def solution(mesh):
    return jax.shard_map(
        per_device,
        mesh=mesh,
        in_specs=(
            P(None, None, ("order", "basin")),
            P(),
            P(),
            P(),
            P(),
            P(("order", "basin")),
            P(("order", "basin")),
            P(("order", "basin"), None),
            P(("order", "basin"), None),
        ),
        out_specs=P(None, ("order", "basin")),
        check_vma=False,
    )
```

```python
import functools

import jax
import jax.numpy as jnp
from jax import lax
from jax.experimental import pallas as pl
from jax.experimental.pallas import tpu as pltpu
from jax.sharding import PartitionSpec as P

F32 = jnp.float32
BF16 = jnp.bfloat16
ID_ROWS = 8
TABLE_ROWS = 16
KNOWN = 5
INFO_ROWS = 8
CHUNK = 512


def vmem():
    return pl.BlockSpec(memory_space=pltpu.VMEM)


def call(body, out_shape, megabytes=8, **more):
    return pl.pallas_call(
        body,
        out_shape=out_shape,
        out_specs=jax.tree.map(lambda _: vmem(), out_shape),
        compiler_params=pltpu.CompilerParams(vmem_limit_bytes=megabytes << 20),
        **more,
    )


def delayed(series, days):
    return jnp.concatenate(
        [jnp.zeros((days, series.shape[1]), series.dtype), series[: series.shape[0] - days]], axis=0
    )


def routing_coefficients(travel_time, weight_x):
    held = travel_time * (1.0 - weight_x)
    denominator = held + 0.5
    coeff_first = (0.5 - travel_time * weight_x) / denominator
    coeff_second = (0.5 + travel_time * weight_x) / denominator
    recession = (held - 0.5) / denominator
    return coeff_first, coeff_first * recession + coeff_second, recession


def route(inflow, coefficients):
    first, later, recession = coefficients
    stored, power, reach = inflow, recession, 1
    while reach < inflow.shape[0]:
        stored = stored + power * delayed(stored, reach)
        power, reach = power * power, 2 * reach
    return first * inflow + later * delayed(stored, 1)


def in_halves(values):
    high = values.astype(BF16)
    return jnp.concatenate([high, (values - high.astype(F32)).astype(BF16)], axis=0)


def choose(values, table):
    both = jnp.dot(in_halves(values), table, preferred_element_type=F32)
    return both[: values.shape[0]] + both[values.shape[0] :]


def as_column(row):
    return jnp.transpose(jnp.broadcast_to(row, (8, row.shape[1])))[:, :1]


def one_hot(index_column, width):
    lanes = lax.broadcasted_iota(jnp.int32, (index_column.shape[0], width), 1).astype(F32)
    return jnp.where(index_column == lanes, 1.0, 0.0).astype(BF16)


def lay_out(ref, rows, first_row=0):
    count = rows.shape[0]
    if len(ref.shape) == 2:
        ref[first_row : first_row + count, :] = rows
    else:
        capacity = ref.shape[2]
        for basin in range(ref.shape[0]):
            ref[basin, first_row : first_row + count, :] = rows[
                :, basin * capacity : (basin + 1) * capacity
            ]


def take_in(ref, first_row, count):
    if len(ref.shape) == 2:
        return ref[first_row : first_row + count, :]
    return jnp.concatenate(
        [ref[basin, first_row : first_row + count, :] for basin in range(ref.shape[0])], axis=1
    )


def send_slots(drain_to, basins, capacity):
    reaches = drain_to.shape[1]
    basin_rows = max(basins, 8)
    member = (lax.broadcasted_iota(jnp.int32, (basin_rows, reaches), 0) == drain_to).astype(F32)
    before = lax.broadcasted_iota(jnp.int32, (reaches, reaches), 0)
    after = lax.broadcasted_iota(jnp.int32, (reaches, reaches), 1)
    upper = jnp.where(before < after, 1.0, 0.0).astype(BF16)
    earlier = jnp.dot(member.astype(BF16), upper, preferred_element_type=F32)
    rank = jnp.sum(member * earlier, axis=0, keepdims=True)
    return drain_to.astype(F32) * capacity + rank


def slot_tables(drain_to, reach, basins, capacity):
    send_table = one_hot(as_column(send_slots(drain_to, basins, capacity)), basins * capacity)
    digits = jnp.concatenate(
        [reach // 16, reach % 16, jnp.zeros((6, reach.shape[1]), jnp.int32)], axis=0
    )
    found = jnp.dot(digits.astype(F32).astype(BF16), send_table, preferred_element_type=F32)
    return send_table, jnp.broadcast_to(
        16.0 * found[0:1] + found[1:2], (ID_ROWS, send_table.shape[1])
    )


def known(drain_basin, drain_reach, travel_time, weight_x):
    rows = (drain_basin.astype(F32), drain_reach.astype(F32))
    rows += routing_coefficients(travel_time, weight_x)
    blank = jnp.zeros((INFO_ROWS - len(rows), travel_time.shape[1]), F32)
    return jnp.concatenate([*rows, blank], axis=0)


def coefficients_of(info):
    return tuple(info[row : row + 1, :] for row in range(2, KNOWN))


def first_body(
    forcings_hbm,
    w_input_hbm,
    w_recur_hbm,
    gate_bias_hbm,
    w_runoff_hbm,
    travel_hbm,
    weight_hbm,
    drain_basin_hbm,
    drain_reach_hbm,
    runoff_ref,
    told_ref,
    spread_ref,
    between_ref,
    above_ref,
    ready_ref,
    paths_ref,
    missing_ref,
    absent_ref,
    send_table_ref,
    targets_ref,
    outgoing_ref,
    forcings_ref,
    w_input_ref,
    w_recur_ref,
    gate_bias_ref,
    w_runoff_ref,
    travel_ref,
    weight_ref,
    drain_basin_ref,
    drain_reach_ref,
    weights,
    sums,
    arrived,
    *,
    days,
    basins,
):
    loads = [
        pltpu.make_async_copy(source, target, arrived.at[number])
        for number, (source, target) in enumerate(
            [
                (w_recur_hbm, w_recur_ref),
                (w_input_hbm, w_input_ref),
                (gate_bias_hbm, gate_bias_ref),
                (w_runoff_hbm, w_runoff_ref),
                (travel_hbm, travel_ref),
                (weight_hbm, weight_ref),
                (drain_basin_hbm, drain_basin_ref),
                (drain_reach_hbm, drain_reach_ref),
                (forcings_hbm, forcings_ref),
            ]
        )
    ]
    for load in loads:
        load.start()
    reaches = forcings_ref.shape[1]
    channels = forcings_ref.shape[0] // days
    units = w_recur_ref.shape[1]
    gates = 4 * units
    per_block = units // channels - 1
    capacity = 2 * reaches // basins
    for day in range(per_block):
        weights[day, units:, :] = jnp.zeros((units, gates), BF16)
    for blank_ref in (between_ref, above_ref, ready_ref, paths_ref, missing_ref, absent_ref):
        blank_ref[...] = jnp.zeros_like(blank_ref)
    for load in loads[:-1]:
        load.wait()

    gate_lane = lax.broadcasted_iota(jnp.int32, (1, gates), 1)
    is_candidate = (gate_lane >= 2 * units) & (gate_lane < 3 * units)
    scale = jnp.where(is_candidate, 1.0, 0.5)
    recur = (jnp.transpose(w_recur_ref[...].astype(F32)) * (0.5 * scale)).astype(BF16)
    inputs = (w_input_ref[...].astype(F32) * scale).astype(BF16)
    thirds = [third.astype(F32) for third in in_thirds(gate_bias_ref[...] * scale)]
    blank = jnp.zeros((channels - len(thirds), gates), F32)
    biases = jnp.concatenate([*thirds, blank], axis=0).astype(BF16)
    readout = as_column(0.5 * w_runoff_ref[...])
    for day in range(per_block):
        weights[day, :units, :] = recur
        weights[day, units + day * channels : units + (day + 1) * channels, :] = inputs
        weights[day, units + per_block * channels :, :] = biases
    chunk = min(CHUNK, reaches)
    chunks = reaches // chunk

    info = known(drain_basin_ref[...], drain_reach_ref[...], travel_ref[...], weight_ref[...])
    told_ref[days:, :] = info
    for basin in range(basins):
        spread_ref[basin] = info
    send_table, targets = slot_tables(drain_basin_ref[...], drain_reach_ref[...], basins, capacity)
    send_table_ref[...] = send_table
    targets_ref[...] = targets
    loads[-1].wait()

    state = [
        (jnp.zeros((chunk, units), BF16), jnp.zeros((chunk, units), F32)) for _ in range(chunks)
    ]
    for first in range(0, days, per_block):
        count = min(per_block, days - first)
        forced = [forcings_ref[first * channels : (first + count) * channels, :]]
        if count < per_block:
            forced.append(jnp.zeros(((per_block - count) * channels, reaches), BF16))
        forced.append(jnp.ones((channels, reaches), BF16))
        forced = jnp.transpose(jnp.concatenate(forced, axis=0))
        for day in range(count):
            for part in range(chunks):
                hidden, memory = state[part]
                span = slice(part * chunk, (part + 1) * chunk)
                gate_sums = jnp.dot(
                    jnp.concatenate([hidden, forced[span]], axis=1),
                    weights[day],
                    preferred_element_type=F32,
                )
                ingate = jnp.tanh(gate_sums[:, :units])
                forget = jnp.tanh(gate_sums[:, units : 2 * units])
                candidate = jnp.tanh(gate_sums[:, 2 * units : 3 * units])
                outgate = jnp.tanh(gate_sums[:, 3 * units :])
                memory = 0.5 * ((forget * memory + memory) + (ingate * candidate + candidate))
                squashed = jnp.tanh(memory)
                hidden = (outgate * squashed + squashed).astype(BF16)
                drained = jnp.sum(
                    jnp.transpose(hidden).astype(F32) * readout, axis=0, keepdims=True
                )
                sums[first + day : first + day + 1, span] = drained
                state[part] = (hidden, memory)
    pre = sums[...]
    runoff = jnp.maximum(pre, 0.0) + jnp.log1p(jnp.exp(-jnp.abs(pre)))
    runoff_ref[...] = runoff
    routed = route(runoff, coefficients_of(info))
    told_ref[:days, :] = routed
    lay_out(outgoing_ref, choose(routed, send_table_ref[...]))
    lay_out(outgoing_ref, targets_ref[...], days)


def unpack_body(received_ref, *arrive_refs):
    days, reaches = arrive_refs[0].shape
    recv_table = one_hot(as_column(take_in(received_ref, days, 1)), reaches)
    arrive = choose(take_in(received_ref, 0, days), recv_table)
    for arrive_ref in arrive_refs:
        arrive_ref[...] = arrive


def route_body(runoff_ref, told_ref, arrive_ref, out_ref):
    info = told_ref[runoff_ref.shape[0] :, :]
    out_ref[...] = route(runoff_ref[...] + arrive_ref[...], coefficients_of(info))


def pack_body(runoff_ref, told_ref, send_table_ref, targets_ref, arrive_ref, outgoing_ref):
    days = runoff_ref.shape[0]
    info = told_ref[days:, :]
    routed = route(runoff_ref[...] + arrive_ref[...], coefficients_of(info))
    lay_out(outgoing_ref, choose(routed, send_table_ref[...]))
    lay_out(outgoing_ref, targets_ref[...], days)


def in_thirds(values):
    high = values.astype(BF16)
    rest = values - high.astype(F32)
    middle = rest.astype(BF16)
    return [high, middle, (rest - middle.astype(F32)).astype(BF16)]


def bundle_body(told_ref, tables_ref, bundle_ref):
    rows = told_ref.shape[0]
    bundle_ref[:rows, :] = told_ref[...]
    for basin in range(tables_ref.shape[0]):
        first = rows + basin * INFO_ROWS
        bundle_ref[first : first + INFO_ROWS, :] = tables_ref[basin]


def info_table(tables):
    pieces = []
    for first in range(0, tables.shape[0], INFO_ROWS):
        info = tables[first : first + INFO_ROWS]
        reach = info[1:2].astype(jnp.int32)
        rows = [info[0:1], (reach // 16).astype(F32), (reach % 16).astype(F32)]
        for row in range(2, KNOWN):
            rows += [third.astype(F32) for third in in_thirds(info[row : row + 1])]
        rows.append(jnp.zeros((TABLE_ROWS - len(rows), reach.shape[1]), F32))
        pieces.append(jnp.concatenate(rows, axis=0).astype(BF16))
    return jnp.concatenate(pieces, axis=0)


def looked_up(table, from_basin, from_reach):
    reaches = table.shape[1]
    sublanes = lax.broadcasted_iota(jnp.int32, (reaches, reaches), 0).astype(F32)
    pick = jnp.where(sublanes == from_reach, 1.0, 0.0).astype(BF16)
    picked = jnp.dot(table, pick, preferred_element_type=F32)
    found = jnp.zeros((TABLE_ROWS, reaches), F32)
    for basin in range(table.shape[0] // TABLE_ROWS):
        here = from_basin == float(basin)
        found = found + jnp.where(here, picked[basin * TABLE_ROWS : (basin + 1) * TABLE_ROWS], 0.0)
    coefficients = tuple(
        (found[row : row + 1] + found[row + 1 : row + 2]) + found[row + 2 : row + 3]
        for row in (3, 6, 9)
    )
    return found[0:1], 16.0 * found[1:2] + found[2:3], coefficients


def by_target(values, to_basin, to_reach, basins):
    days, reaches = values.shape
    halves = in_halves(values).astype(F32)
    parts = [
        jnp.where(to_basin == float(basin), halves, 0.0).astype(BF16) for basin in range(basins)
    ]
    table = one_hot(as_column(to_reach), reaches)
    sums = jnp.dot(jnp.concatenate(parts, axis=0), table, preferred_element_type=F32)
    return [
        sums[first : first + days] + sums[first + days : first + 2 * days]
        for first in range(0, 2 * basins * days, 2 * days)
    ]


def prepare_body(between_ref, above_ref, ready_ref, paths_ref):
    basins, days, reaches = ready_ref.shape
    rows = days + INFO_ROWS
    to_basin, to_reach, coefficients = looked_up(
        info_table(between_ref[rows:, :]), above_ref[days : days + 1, :], above_ref[days + 1 : days + 2, :]
    )
    paths_ref[:rows, :] = above_ref[...]
    blank = jnp.zeros((INFO_ROWS - KNOWN, reaches), F32)
    paths_ref[rows:, :] = jnp.concatenate([to_basin, to_reach, *coefficients, blank], axis=0)
    own = between_ref[days:rows, :]
    for basin, sums in enumerate(by_target(between_ref[:days, :], own[0:1], own[1:2], basins)):
        ready_ref[basin] = sums


def pack_beyond_body(passed_ref, ready_ref, paths_ref, outgoing_ref):
    basins, days, _ = outgoing_ref.shape
    above, between = paths_ref[days : days + INFO_ROWS, :], paths_ref[days + INFO_ROWS :, :]
    outflow = paths_ref[:days, :] + route(passed_ref[...], coefficients_of(above))
    routed = route(outflow, coefficients_of(between))
    for basin, sums in enumerate(by_target(routed, between[0:1], between[1:2], basins)):
        outgoing_ref[basin] = ready_ref[basin] + sums


def add_up_body(received_ref, arrive_ref):
    total = received_ref[0]
    for basin in range(1, received_ref.shape[0]):
        total = total + received_ref[basin]
    arrive_ref[...] = total


def per_device(
    forcings, w_input, w_recur, gate_bias, w_runoff, travel_time, weight_x, drain_basin, drain_reach
):
    basins = lax.axis_size("basin")
    groups = lax.axis_size("order")
    days, channels, reaches = forcings.shape
    units = w_recur.shape[1]
    capacity = 2 * reaches // basins
    slots = basins * capacity
    split = capacity % 128 == 0

    def series():
        return jax.ShapeDtypeStruct((days, reaches), F32)

    def swap(outgoing):
        return lax.all_to_all(outgoing, "basin", split_axis=0, concat_axis=0, tiled=True)

    def exchange(outgoing):
        if split:
            return swap(outgoing)
        outgoing = outgoing.reshape(-1, basins, capacity)
        received = lax.all_to_all(outgoing, "basin", split_axis=1, concat_axis=1, tiled=True)
        return received.reshape(-1, slots)

    def row(values):
        return values.reshape(1, -1)

    operands = (
        forcings.reshape(days * channels, reaches),
        w_input.T,
        w_recur,
        row(gate_bias),
        row(w_runoff),
        row(travel_time),
        row(weight_x),
        row(drain_basin),
        row(drain_reach),
    )
    told_shape = jax.ShapeDtypeStruct((days + INFO_ROWS, reaches), F32)
    bundle_shape = jax.ShapeDtypeStruct((days + (1 + basins) * INFO_ROWS, reaches), F32)
    ready_shape = jax.ShapeDtypeStruct((basins, days, reaches), F32)
    paths_shape = jax.ShapeDtypeStruct((days + 2 * INFO_ROWS, reaches), F32)
    payload_shape = jax.ShapeDtypeStruct(
        (basins, days + ID_ROWS, capacity) if split else (days + ID_ROWS, slots), F32
    )
    runoff, told, spread, between, above, ready, paths, *late = call(
        functools.partial(first_body, days=days, basins=basins),
        [
            series(),
            told_shape,
            jax.ShapeDtypeStruct((basins, INFO_ROWS, reaches), F32),
            bundle_shape,
            told_shape,
            ready_shape,
            paths_shape,
            series(),
            series(),
            jax.ShapeDtypeStruct((reaches, slots), BF16),
            jax.ShapeDtypeStruct((ID_ROWS, slots), F32),
            payload_shape,
        ],
        megabytes=56,
        in_specs=[pl.BlockSpec(memory_space=pltpu.HBM) for _ in operands],
        scratch_shapes=[pltpu.VMEM(array.shape, array.dtype) for array in operands]
        + [
            pltpu.VMEM((units // channels - 1, 2 * units, 4 * units), BF16),
            pltpu.VMEM((days, reaches), F32),
            pltpu.SemaphoreType.DMA((len(operands),)),
        ],
    )(*operands)

    missing, absent, send_table, targets, outgoing = late
    group = lax.axis_index("order")
    later = range(1, groups // 2)

    def moved(block, routes):
        pairs = [
            (source * basins + basin, target * basins + basin)
            for source, target in routes
            for basin in range(basins)
        ]
        return lax.ppermute(block, ("order", "basin"), pairs)

    neighbours = [(place, place ^ 1) for place in range(groups)]
    two_down = [(place, (place + 2) % groups) for place in range(groups)]

    def nothing(*_):
        return jnp.zeros((days, reaches), F32)

    above = lax.cond(
        group % 2 == 1, lambda told, blank: moved(told, two_down), lambda _, blank: blank, told, above
    )
    spread, above = lax.optimization_barrier((spread, above))
    between = lax.cond(
        (group % 2 == 0) & (group > 1),
        lambda spread, told, _: call(bundle_body, bundle_shape)(told, swap(spread)),
        lambda spread, told, blank: blank,
        spread,
        told,
        between,
    )
    outgoing, between = lax.optimization_barrier((outgoing, between))

    def deliver(outgoing, copies=1):
        return tuple(call(unpack_body, [series()] * copies)(exchange(outgoing)))

    arrive, passed = lax.cond(
        group == 0,
        lambda outgoing, *_: deliver(outgoing, 2),
        lambda outgoing, *blanks: tuple(blanks),
        outgoing,
        missing,
        absent,
    )
    arrive, passed, between = lax.optimization_barrier((arrive, passed, between))
    passed = moved(passed, [(place, place ^ 3) for place in range(groups)])
    between = lax.cond(
        group > 1, lambda told: moved(told, neighbours), lambda told: told, between
    )
    ready, paths = lax.cond(
        (group % 2 == 1) & (group > 1),
        lambda *known: tuple(call(prepare_body, [ready_shape, paths_shape], 24)(*known[:2])),
        lambda between, above, ready, paths: (ready, paths),
        between,
        above,
        ready,
        paths,
    )
    arrive, ready = lax.optimization_barrier((arrive, ready))
    arrive = lax.cond(
        group < 2, lambda arrive: moved(arrive, neighbours), lambda arrive: arrive, arrive
    )
    arrive = jnp.where(group == 1, arrive, 0.0)
    for pair in later:
        above, between, below = 2 * pair - 1, 2 * pair, 2 * pair + 1
        if pair > 1:
            passed = moved(arrive, two_down)
        delivered = lax.cond(
            group == above,
            lambda arrive: deliver(
                call(pack_body, payload_shape)(runoff, told, send_table, targets, arrive)
            )[0],
            nothing,
            arrive,
        )
        passed, delivered = lax.optimization_barrier((passed, delivered))
        received = lax.cond(
            group == below,
            lambda passed, _: call(add_up_body, series())(
                swap(call(pack_beyond_body, ready_shape, 24)(passed, ready, paths))
            ),
            lambda _, delivered: delivered,
            passed,
            delivered,
        )
        received = lax.cond(
            (group == above) | (group == between),
            lambda received: moved(received, [(above, between)]),
            lambda received: received,
            received,
        )
        arrive = arrive + jnp.where(group == above, 0.0, received)
    return call(route_body, series())(runoff, told, arrive)


def solution(mesh):
    return jax.shard_map(
        per_device,
        mesh=mesh,
        in_specs=(
            P(None, None, ("order", "basin")),
            P(),
            P(),
            P(),
            P(),
            P(("order", "basin")),
            P(("order", "basin")),
            P(("order", "basin"), None),
            P(("order", "basin"), None),
        ),
        out_specs=P(None, ("order", "basin")),
        check_vma=False,
    )
```

```python
import functools

import jax
import jax.numpy as jnp
from jax import lax
from jax.experimental import pallas as pl
from jax.experimental.pallas import tpu as pltpu
from jax.sharding import PartitionSpec as P

F32 = jnp.float32
BF16 = jnp.bfloat16
ID_ROWS = 8
TABLE_ROWS = 16
KNOWN = 5
INFO_ROWS = 8
CHUNK = 512


def vmem():
    return pl.BlockSpec(memory_space=pltpu.VMEM)


def call(body, out_shape, megabytes=8, **more):
    return pl.pallas_call(
        body,
        out_shape=out_shape,
        out_specs=jax.tree.map(lambda _: vmem(), out_shape),
        compiler_params=pltpu.CompilerParams(vmem_limit_bytes=megabytes << 20),
        **more,
    )


def delayed(series, days):
    return jnp.concatenate(
        [jnp.zeros((days, series.shape[1]), series.dtype), series[: series.shape[0] - days]], axis=0
    )


def routing_coefficients(travel_time, weight_x):
    held = travel_time * (1.0 - weight_x)
    denominator = held + 0.5
    coeff_first = (0.5 - travel_time * weight_x) / denominator
    coeff_second = (0.5 + travel_time * weight_x) / denominator
    recession = (held - 0.5) / denominator
    return coeff_first, coeff_first * recession + coeff_second, recession


def route(inflow, coefficients):
    first, later, recession = coefficients
    stored, power, reach = inflow, recession, 1
    while reach < inflow.shape[0]:
        stored = stored + power * delayed(stored, reach)
        power, reach = power * power, 2 * reach
    return first * inflow + later * delayed(stored, 1)


def in_halves(values):
    high = values.astype(BF16)
    return jnp.concatenate([high, (values - high.astype(F32)).astype(BF16)], axis=0)


def choose(values, table):
    both = jnp.dot(in_halves(values), table, preferred_element_type=F32)
    return both[: values.shape[0]] + both[values.shape[0] :]


def as_column(row):
    return jnp.transpose(jnp.broadcast_to(row, (8, row.shape[1])))[:, :1]


def one_hot(index_column, width):
    lanes = lax.broadcasted_iota(jnp.int32, (index_column.shape[0], width), 1).astype(F32)
    return jnp.where(index_column == lanes, 1.0, 0.0).astype(BF16)


def lay_out(ref, rows, first_row=0):
    count = rows.shape[0]
    if len(ref.shape) == 2:
        ref[first_row : first_row + count, :] = rows
    else:
        capacity = ref.shape[2]
        for basin in range(ref.shape[0]):
            ref[basin, first_row : first_row + count, :] = rows[
                :, basin * capacity : (basin + 1) * capacity
            ]


def take_in(ref, first_row, count):
    if len(ref.shape) == 2:
        return ref[first_row : first_row + count, :]
    return jnp.concatenate(
        [ref[basin, first_row : first_row + count, :] for basin in range(ref.shape[0])], axis=1
    )


def send_slots(drain_to, basins, capacity):
    reaches = drain_to.shape[1]
    basin_rows = max(basins, 8)
    member = (lax.broadcasted_iota(jnp.int32, (basin_rows, reaches), 0) == drain_to).astype(F32)
    before = lax.broadcasted_iota(jnp.int32, (reaches, reaches), 0)
    after = lax.broadcasted_iota(jnp.int32, (reaches, reaches), 1)
    upper = jnp.where(before < after, 1.0, 0.0).astype(BF16)
    earlier = jnp.dot(member.astype(BF16), upper, preferred_element_type=F32)
    rank = jnp.sum(member * earlier, axis=0, keepdims=True)
    return drain_to.astype(F32) * capacity + rank


def slot_tables(drain_to, reach, basins, capacity):
    send_table = one_hot(as_column(send_slots(drain_to, basins, capacity)), basins * capacity)
    digits = jnp.concatenate(
        [reach // 16, reach % 16, jnp.zeros((6, reach.shape[1]), jnp.int32)], axis=0
    )
    found = jnp.dot(digits.astype(F32).astype(BF16), send_table, preferred_element_type=F32)
    return send_table, jnp.broadcast_to(
        16.0 * found[0:1] + found[1:2], (ID_ROWS, send_table.shape[1])
    )


def known(drain_basin, drain_reach, travel_time, weight_x):
    rows = (drain_basin.astype(F32), drain_reach.astype(F32))
    rows += routing_coefficients(travel_time, weight_x)
    blank = jnp.zeros((INFO_ROWS - len(rows), travel_time.shape[1]), F32)
    return jnp.concatenate([*rows, blank], axis=0)


def coefficients_of(info):
    return tuple(info[row : row + 1, :] for row in range(2, KNOWN))


def first_body(
    forcings_hbm,
    w_input_hbm,
    w_recur_hbm,
    gate_bias_hbm,
    w_runoff_hbm,
    travel_hbm,
    weight_hbm,
    drain_basin_hbm,
    drain_reach_hbm,
    runoff_ref,
    told_ref,
    spread_ref,
    between_ref,
    above_ref,
    ready_ref,
    paths_ref,
    pick_ref,
    missing_ref,
    absent_ref,
    send_table_ref,
    targets_ref,
    outgoing_ref,
    forcings_ref,
    w_input_ref,
    w_recur_ref,
    gate_bias_ref,
    w_runoff_ref,
    travel_ref,
    weight_ref,
    drain_basin_ref,
    drain_reach_ref,
    weights,
    sums,
    arrived,
    *,
    days,
    basins,
):
    loads = [
        pltpu.make_async_copy(source, target, arrived.at[number])
        for number, (source, target) in enumerate(
            [
                (w_recur_hbm, w_recur_ref),
                (w_input_hbm, w_input_ref),
                (gate_bias_hbm, gate_bias_ref),
                (w_runoff_hbm, w_runoff_ref),
                (travel_hbm, travel_ref),
                (weight_hbm, weight_ref),
                (drain_basin_hbm, drain_basin_ref),
                (drain_reach_hbm, drain_reach_ref),
                (forcings_hbm, forcings_ref),
            ]
        )
    ]
    for load in loads:
        load.start()
    reaches = forcings_ref.shape[1]
    channels = forcings_ref.shape[0] // days
    units = w_recur_ref.shape[1]
    gates = 4 * units
    per_block = units // channels - 1
    capacity = 2 * reaches // basins
    for day in range(per_block):
        weights[day, units:, :] = jnp.zeros((units, gates), BF16)
    blanks = (between_ref, above_ref, ready_ref, paths_ref, pick_ref, missing_ref, absent_ref)
    for blank_ref in blanks:
        blank_ref[...] = jnp.zeros_like(blank_ref)
    for load in loads[:-1]:
        load.wait()

    gate_lane = lax.broadcasted_iota(jnp.int32, (1, gates), 1)
    is_candidate = (gate_lane >= 2 * units) & (gate_lane < 3 * units)
    scale = jnp.where(is_candidate, 1.0, 0.5)
    recur = (jnp.transpose(w_recur_ref[...].astype(F32)) * (0.5 * scale)).astype(BF16)
    inputs = (w_input_ref[...].astype(F32) * scale).astype(BF16)
    thirds = [third.astype(F32) for third in in_thirds(gate_bias_ref[...] * scale)]
    blank = jnp.zeros((channels - len(thirds), gates), F32)
    biases = jnp.concatenate([*thirds, blank], axis=0).astype(BF16)
    readout = as_column(0.5 * w_runoff_ref[...])
    for day in range(per_block):
        weights[day, :units, :] = recur
        weights[day, units + day * channels : units + (day + 1) * channels, :] = inputs
        weights[day, units + per_block * channels :, :] = biases
    chunk = min(CHUNK, reaches)
    chunks = reaches // chunk

    info = known(drain_basin_ref[...], drain_reach_ref[...], travel_ref[...], weight_ref[...])
    told_ref[days:, :] = info
    for basin in range(basins):
        spread_ref[basin] = info
    send_table, targets = slot_tables(drain_basin_ref[...], drain_reach_ref[...], basins, capacity)
    send_table_ref[...] = send_table
    targets_ref[...] = targets
    loads[-1].wait()

    state = [
        (jnp.zeros((chunk, units), BF16), jnp.zeros((chunk, units), F32)) for _ in range(chunks)
    ]
    for first in range(0, days, per_block):
        count = min(per_block, days - first)
        forced = [forcings_ref[first * channels : (first + count) * channels, :]]
        if count < per_block:
            forced.append(jnp.zeros(((per_block - count) * channels, reaches), BF16))
        forced.append(jnp.ones((channels, reaches), BF16))
        forced = jnp.transpose(jnp.concatenate(forced, axis=0))
        for day in range(count):
            for part in range(chunks):
                hidden, memory = state[part]
                span = slice(part * chunk, (part + 1) * chunk)
                gate_sums = jnp.dot(
                    jnp.concatenate([hidden, forced[span]], axis=1),
                    weights[day],
                    preferred_element_type=F32,
                )
                ingate = jnp.tanh(gate_sums[:, :units])
                forget = jnp.tanh(gate_sums[:, units : 2 * units])
                candidate = jnp.tanh(gate_sums[:, 2 * units : 3 * units])
                outgate = jnp.tanh(gate_sums[:, 3 * units :])
                memory = 0.5 * ((forget * memory + memory) + (ingate * candidate + candidate))
                squashed = jnp.tanh(memory)
                hidden = (outgate * squashed + squashed).astype(BF16)
                drained = jnp.sum(
                    jnp.transpose(hidden).astype(F32) * readout, axis=0, keepdims=True
                )
                sums[first + day : first + day + 1, span] = drained
                state[part] = (hidden, memory)
    pre = sums[...]
    runoff = jnp.maximum(pre, 0.0) + jnp.log1p(jnp.exp(-jnp.abs(pre)))
    runoff_ref[...] = runoff
    routed = route(runoff, coefficients_of(info))
    told_ref[:days, :] = routed
    lay_out(outgoing_ref, choose(routed, send_table_ref[...]))
    lay_out(outgoing_ref, targets_ref[...], days)


def unpack_body(received_ref, *arrive_refs):
    days, reaches = arrive_refs[0].shape
    recv_table = one_hot(as_column(take_in(received_ref, days, 1)), reaches)
    arrive = choose(take_in(received_ref, 0, days), recv_table)
    for arrive_ref in arrive_refs:
        arrive_ref[...] = arrive


def route_body(runoff_ref, told_ref, arrive_ref, out_ref):
    info = told_ref[runoff_ref.shape[0] :, :]
    out_ref[...] = route(runoff_ref[...] + arrive_ref[...], coefficients_of(info))


def pack_body(runoff_ref, told_ref, send_table_ref, targets_ref, arrive_ref, outgoing_ref):
    days = runoff_ref.shape[0]
    info = told_ref[days:, :]
    routed = route(runoff_ref[...] + arrive_ref[...], coefficients_of(info))
    lay_out(outgoing_ref, choose(routed, send_table_ref[...]))
    lay_out(outgoing_ref, targets_ref[...], days)


def in_thirds(values):
    high = values.astype(BF16)
    rest = values - high.astype(F32)
    middle = rest.astype(BF16)
    return [high, middle, (rest - middle.astype(F32)).astype(BF16)]


def bundle_body(told_ref, tables_ref, bundle_ref):
    rows = told_ref.shape[0]
    bundle_ref[:rows, :] = told_ref[...]
    bundle_ref[rows:, :] = jnp.concatenate(
        [tables_ref[basin, :KNOWN, :] for basin in range(tables_ref.shape[0])], axis=0
    )


def info_table(tables):
    pieces = []
    for first in range(0, tables.shape[0], KNOWN):
        info = tables[first : first + KNOWN]
        reach = info[1:2].astype(jnp.int32)
        rows = [info[0:1], (reach // 16).astype(F32), (reach % 16).astype(F32)]
        for row in range(2, KNOWN):
            rows += [third.astype(F32) for third in in_thirds(info[row : row + 1])]
        rows.append(jnp.zeros((TABLE_ROWS - len(rows), reach.shape[1]), F32))
        pieces.append(jnp.concatenate(rows, axis=0).astype(BF16))
    return jnp.concatenate(pieces, axis=0)


def pick_body(above_ref, pick_ref):
    reaches = pick_ref.shape[1]
    days = above_ref.shape[0] - INFO_ROWS
    sublanes = lax.broadcasted_iota(jnp.int32, (reaches, reaches), 0).astype(F32)
    pick_ref[...] = jnp.where(sublanes == above_ref[days + 1 : days + 2, :], 1.0, 0.0).astype(BF16)


def looked_up(table, from_basin, pick):
    reaches = table.shape[1]
    picked = jnp.dot(table, pick, preferred_element_type=F32)
    found = jnp.zeros((TABLE_ROWS, reaches), F32)
    for basin in range(table.shape[0] // TABLE_ROWS):
        here = from_basin == float(basin)
        found = found + jnp.where(here, picked[basin * TABLE_ROWS : (basin + 1) * TABLE_ROWS], 0.0)
    coefficients = tuple(
        (found[row : row + 1] + found[row + 1 : row + 2]) + found[row + 2 : row + 3]
        for row in (3, 6, 9)
    )
    return found[0:1], 16.0 * found[1:2] + found[2:3], coefficients


def by_target(values, to_basin, to_reach, basins):
    days, reaches = values.shape
    halves = in_halves(values).astype(F32)
    parts = [
        jnp.where(to_basin == float(basin), halves, 0.0).astype(BF16) for basin in range(basins)
    ]
    table = one_hot(as_column(to_reach), reaches)
    sums = jnp.dot(jnp.concatenate(parts, axis=0), table, preferred_element_type=F32)
    return [
        sums[first : first + days] + sums[first + days : first + 2 * days]
        for first in range(0, 2 * basins * days, 2 * days)
    ]


def prepare_body(between_ref, above_ref, pick_ref, ready_ref, paths_ref):
    basins, days, reaches = ready_ref.shape
    rows = days + INFO_ROWS
    to_basin, to_reach, coefficients = looked_up(
        info_table(between_ref[rows:, :]), above_ref[days : days + 1, :], pick_ref[...]
    )
    paths_ref[:rows, :] = above_ref[...]
    blank = jnp.zeros((INFO_ROWS - KNOWN, reaches), F32)
    paths_ref[rows:, :] = jnp.concatenate([to_basin, to_reach, *coefficients, blank], axis=0)
    own = between_ref[days:rows, :]
    for basin, sums in enumerate(by_target(between_ref[:days, :], own[0:1], own[1:2], basins)):
        ready_ref[basin] = sums


def pack_beyond_body(passed_ref, ready_ref, paths_ref, outgoing_ref):
    basins, days, _ = outgoing_ref.shape
    above, between = paths_ref[days : days + INFO_ROWS, :], paths_ref[days + INFO_ROWS :, :]
    outflow = paths_ref[:days, :] + route(passed_ref[...], coefficients_of(above))
    routed = route(outflow, coefficients_of(between))
    for basin, sums in enumerate(by_target(routed, between[0:1], between[1:2], basins)):
        outgoing_ref[basin] = ready_ref[basin] + sums


def add_up_body(received_ref, arrive_ref):
    total = received_ref[0]
    for basin in range(1, received_ref.shape[0]):
        total = total + received_ref[basin]
    arrive_ref[...] = total


def per_device(
    forcings, w_input, w_recur, gate_bias, w_runoff, travel_time, weight_x, drain_basin, drain_reach
):
    basins = lax.axis_size("basin")
    groups = lax.axis_size("order")
    days, channels, reaches = forcings.shape
    units = w_recur.shape[1]
    capacity = 2 * reaches // basins
    slots = basins * capacity
    split = capacity % 128 == 0

    def series():
        return jax.ShapeDtypeStruct((days, reaches), F32)

    def swap(outgoing):
        return lax.all_to_all(outgoing, "basin", split_axis=0, concat_axis=0, tiled=True)

    def exchange(outgoing):
        if split:
            return swap(outgoing)
        outgoing = outgoing.reshape(-1, basins, capacity)
        received = lax.all_to_all(outgoing, "basin", split_axis=1, concat_axis=1, tiled=True)
        return received.reshape(-1, slots)

    def row(values):
        return values.reshape(1, -1)

    operands = (
        forcings.reshape(days * channels, reaches),
        w_input.T,
        w_recur,
        row(gate_bias),
        row(w_runoff),
        row(travel_time),
        row(weight_x),
        row(drain_basin),
        row(drain_reach),
    )
    told_shape = jax.ShapeDtypeStruct((days + INFO_ROWS, reaches), F32)
    bundle_shape = jax.ShapeDtypeStruct((days + INFO_ROWS + basins * KNOWN, reaches), F32)
    ready_shape = jax.ShapeDtypeStruct((basins, days, reaches), F32)
    pick_shape = jax.ShapeDtypeStruct((reaches, reaches), BF16)
    paths_shape = jax.ShapeDtypeStruct((days + 2 * INFO_ROWS, reaches), F32)
    payload_shape = jax.ShapeDtypeStruct(
        (basins, days + ID_ROWS, capacity) if split else (days + ID_ROWS, slots), F32
    )
    runoff, told, spread, between, above, ready, paths, pick, *late = call(
        functools.partial(first_body, days=days, basins=basins),
        [
            series(),
            told_shape,
            jax.ShapeDtypeStruct((basins, INFO_ROWS, reaches), F32),
            bundle_shape,
            told_shape,
            ready_shape,
            paths_shape,
            pick_shape,
            series(),
            series(),
            jax.ShapeDtypeStruct((reaches, slots), BF16),
            jax.ShapeDtypeStruct((ID_ROWS, slots), F32),
            payload_shape,
        ],
        megabytes=56,
        in_specs=[pl.BlockSpec(memory_space=pltpu.HBM) for _ in operands],
        scratch_shapes=[pltpu.VMEM(array.shape, array.dtype) for array in operands]
        + [
            pltpu.VMEM((units // channels - 1, 2 * units, 4 * units), BF16),
            pltpu.VMEM((days, reaches), F32),
            pltpu.SemaphoreType.DMA((len(operands),)),
        ],
    )(*operands)

    missing, absent, send_table, targets, outgoing = late
    group = lax.axis_index("order")
    later = range(1, groups // 2)

    def moved(block, routes):
        pairs = [
            (source * basins + basin, target * basins + basin)
            for source, target in routes
            for basin in range(basins)
        ]
        return lax.ppermute(block, ("order", "basin"), pairs)

    neighbours = [(place, place ^ 1) for place in range(groups)]
    two_down = [(place, (place + 2) % groups) for place in range(groups)]

    def nothing(*_):
        return jnp.zeros((days, reaches), F32)

    above = lax.cond(
        group % 2 == 1, lambda told, blank: moved(told, two_down), lambda _, blank: blank, told, above
    )
    pick = lax.cond(
        (group % 2 == 1) & (group > 1),
        lambda above, _: call(pick_body, pick_shape)(above),
        lambda above, blank: blank,
        above,
        pick,
    )
    spread, above, pick = lax.optimization_barrier((spread, above, pick))
    between = lax.cond(
        (group % 2 == 0) & (group > 1),
        lambda spread, told, _: call(bundle_body, bundle_shape)(told, swap(spread)),
        lambda spread, told, blank: blank,
        spread,
        told,
        between,
    )
    outgoing, between = lax.optimization_barrier((outgoing, between))

    def deliver(outgoing, copies=1):
        return tuple(call(unpack_body, [series()] * copies)(exchange(outgoing)))

    arrive, passed = lax.cond(
        group == 0,
        lambda outgoing, *_: deliver(outgoing, 2),
        lambda outgoing, *blanks: tuple(blanks),
        outgoing,
        missing,
        absent,
    )
    arrive, passed, between = lax.optimization_barrier((arrive, passed, between))
    passed = moved(passed, [(place, place ^ 3) for place in range(groups)])
    between = lax.cond(
        group > 1, lambda told: moved(told, neighbours), lambda told: told, between
    )
    ready, paths = lax.cond(
        (group % 2 == 1) & (group > 1),
        lambda *known: tuple(call(prepare_body, [ready_shape, paths_shape], 24)(*known[:3])),
        lambda between, above, pick, ready, paths: (ready, paths),
        between,
        above,
        pick,
        ready,
        paths,
    )
    arrive, ready = lax.optimization_barrier((arrive, ready))
    arrive = lax.cond(
        group < 2, lambda arrive: moved(arrive, neighbours), lambda arrive: arrive, arrive
    )
    arrive = jnp.where(group == 1, arrive, 0.0)
    for pair in later:
        above, between, below = 2 * pair - 1, 2 * pair, 2 * pair + 1
        if pair > 1:
            passed = moved(arrive, two_down)
        delivered = lax.cond(
            group == above,
            lambda arrive: deliver(
                call(pack_body, payload_shape)(runoff, told, send_table, targets, arrive)
            )[0],
            nothing,
            arrive,
        )
        passed, delivered = lax.optimization_barrier((passed, delivered))
        received = lax.cond(
            group == below,
            lambda passed, _: call(add_up_body, series())(
                swap(call(pack_beyond_body, ready_shape, 24)(passed, ready, paths))
            ),
            lambda _, delivered: delivered,
            passed,
            delivered,
        )
        received = lax.cond(
            (group == above) | (group == between),
            lambda received: moved(received, [(above, between)]),
            lambda received: received,
            received,
        )
        arrive = arrive + jnp.where(group == above, 0.0, received)
    return call(route_body, series())(runoff, told, arrive)


def solution(mesh):
    return jax.shard_map(
        per_device,
        mesh=mesh,
        in_specs=(
            P(None, None, ("order", "basin")),
            P(),
            P(),
            P(),
            P(),
            P(("order", "basin")),
            P(("order", "basin")),
            P(("order", "basin"), None),
            P(("order", "basin"), None),
        ),
        out_specs=P(None, ("order", "basin")),
        check_vma=False,
    )
```
